32 devices in a mesh: groups: 2 (over y), seq: 4 (over z), tp: 2 (over x), dp: 2 (over core).
Axes of the slice: x: 2, y: 2, z: 4, core: 2. Of those that a mesh axis runs over, the one named last changes fastest.
Arguments:
- byte_rows: bfloat16 [16384, 1024], P(('groups', 'seq', 'dp')), parts along dimension 0, may hold values from -80 to 80
- patch_lengths: int32 [16, 128], P(('groups', 'seq', 'dp')), parts along dimension 0, may hold values from 1 to 32, 1024 in all within a row
- patch_owner: int32 [2048, 1], P(('groups', 'seq', 'dp')), parts along dimension 0, may hold values from 0 to 7; in each aligned block of 128 rows (0 to 127, 128 to 255, ...) at most 32 rows name the same one
- patch_stream: bfloat16 [4096, 4096], P(('groups', 'seq', 'dp'), 'tp'), parts along dimension 0, may hold values from -80 to 80
- w_in: bfloat16 [1024, 4096], P(('seq', 'dp'), 'tp'), may hold values from -0.1875 to 0.1875
- norm_gain: float32 [4096], P('tp'), may hold values from 0.1 to 1.9
- w_kv: bfloat16 [2, 4096, 1024], P(None, 'tp', ('seq', 'dp')), may hold values from -0.09375 to 0.09375
- w_query: bfloat16 [1024, 1024], P(None, 'tp'), may hold values from -0.1875 to 0.1875
- w_out: bfloat16 [1024, 1024], P(None, 'tp'), may hold values from -0.1875 to 0.1875
Outputs:
- decoded: bfloat16 [16384, 1024], P(('groups', 'seq', 'dp'), 'tp'), parts along dimension 0
The draws below stay inside these ranges and needn't reach their ends.
There are 2 independent parts, one for each index of `groups`. The reference program is written for one: setup_inputs(seed, part) draws one part's arguments, and reference() takes and returns one part's arrays. A program takes and returns all parts, laid end to end along the dimension named above; an argument that names none is the same for every part. Nothing has to cross between parts.
Inputs may be any that keep to these rules, and one draw needn't show every extreme that they name: `patch_lengths`: row b gives the lengths of the 128 patches that begin and end inside byte block b; every row sums to 1024. `patch_owner`: owners are numbered in the order of seq then dp. Among the 128 patches of one byte block no owner appears more than 32 times, a bound that some block reaches; every owner has some patch.
All inputs are finite; a program needn't handle non-finite values.
Results may differ from the reference program's by a relative error of at most 0.0051.
Values may be sent and summed in bfloat16 or wider, within the bound.
A program may use at most 64 MiB of HBM per device.

```python
import math
import jax
import jax.numpy as jnp
import numpy as np
from jax import lax

D = 4096
DL = 1024
HEAD_DIM = 64
BYTE_DEV = 1024
MAXLEN = 32
WIN = 8
PATCH_DEV = 128
CAP = 32
SLOTS = 256
BYTES = 8192
PATCHES = 1024
N_SEQ = 4
N_DP = 2


def draw_byte_rows(key, part):
    key = jax.random.fold_in(key, 11)
    first = jax.random.fold_in(key, 0)
    values = jax.random.truncated_normal(first, -6.0, 6.0, (BYTES, DL), jnp.float32)
    return values.astype(jnp.bfloat16)


def column_scales(key, rise):
    position = jnp.arange(D, dtype=jnp.float32) / D
    rough = jax.random.uniform(key, (D,), minval=1.0, maxval=2.0)
    return 0.6 * jnp.exp(position * math.log(rise)) * rough


def draw_patch_stream(key, part):
    key = jax.random.fold_in(key, 23)
    first, second = jax.random.split(key, 2)
    rows_total = N_SEQ * N_DP * SLOTS
    values = jax.random.truncated_normal(first, -6.0, 6.0, (rows_total, D), jnp.float32)
    values = values * column_scales(second, 4.0)[None, :]
    return values.astype(jnp.bfloat16)


def levels(stream_key, shape, cuts, smallest, largest):
    def one(dim, parts):
        heights = jax.random.uniform(jax.random.fold_in(jax.random.fold_in(stream_key, 6), dim), (parts,), jnp.float32, smallest / len(cuts), largest / len(cuts))
        return jnp.repeat(jnp.exp(heights), shape[dim] // parts).reshape((-1,) + (1,) * (len(shape) - dim - 1))

    level = one(*cuts[0])
    for cut in cuts[1:]:
        level = level * one(*cut)
    return level


def split_up(count, total, bound, slope):
    weights = [(1 << 20) // math.isqrt(rank ** slope) + 1 for rank in range(2, count + 1)]
    rest, counts = total - bound - (count - 1), [1] * (count - 1)
    while rest > 0:
        free = [i for i in range(count - 1) if counts[i] < bound]
        pool, remaining = sum([weights[i] for i in free]), rest
        for i in free:
            more = min(bound - counts[i], max(1, remaining * weights[i] // pool), rest)
            counts[i] = counts[i] + more
            rest = rest - more
    return np.array([bound] + counts)


def ragged_sizes(rng, amount, total, reach, lean):
    if amount == 2:
        one = jax.random.randint(rng, (), max(1, total - reach), min(reach, total - 1) + 1)
        return jnp.stack([one, total - one])
    sizes = jnp.asarray(split_up(amount, total, reach, lean), jnp.int32)
    twos = (amount - 1) // 2
    donor, receiver = sizes[1:1 + 2 * twos:2], sizes[2:2 + 2 * twos:2]
    margin = jnp.minimum(donor - 1, reach - receiver)
    shifted = jax.random.randint(jax.random.fold_in(rng, 1), (twos,), 0, 1 << 20) % (margin + 1)
    sizes = sizes.at[1:1 + 2 * twos:2].set(donor - shifted).at[2:2 + 2 * twos:2].set(receiver + shifted)
    return sizes[jax.random.permutation(jax.random.fold_in(rng, 2), amount)]


def shared_out(key, own, number, rows, amount, top, most, lean):
    order = jax.random.permutation(key, amount)
    heavy_load, common = shares(amount, rows * top, most, lean, True), shares(amount, rows * top, most, lean, False)
    places = jnp.arange(amount)

    def named(sizes, turn):
        used = int((sizes > 0).sum())
        fixed = max(1, used // 4)
        passed = fixed + (places - fixed + turn * (used - fixed)) % max(1, amount - fixed)
        return jnp.zeros((amount,), jnp.int32).at[order[jnp.where(places < fixed, places, passed)]].set(jnp.asarray(sizes, jnp.int32))

    sizes = jnp.where(number % 4 == 0, named(heavy_load, number // 4), named(common, number - number // 4 - 1))
    mixed = jax.random.permutation(jax.random.fold_in(own, 3), amount)
    giver, receiver = mixed[0:amount // 2 * 2:2], mixed[1:amount // 2 * 2:2]
    room = jnp.minimum(sizes[giver] - 1, most - sizes[receiver]) // 2
    room = jnp.where((giver == order[0]) | (receiver == order[0]) | (sizes[receiver] == 0), 0, jnp.maximum(room, 0))
    passed = jax.random.randint(jax.random.fold_in(own, 4), (amount // 2,), 0, 1 << 20) % (room + 1)
    sizes = sizes.at[giver].add(-passed).at[receiver].add(passed)
    items = jnp.searchsorted(jnp.cumsum(sizes), jnp.arange(rows * top), side="right").astype(jnp.int32)
    grid = items.reshape(top, rows).T
    grid = grid[jax.random.permutation(jax.random.fold_in(own, 1), rows)]
    turn = jax.random.randint(jax.random.fold_in(own, 2), (rows, 1), 0, top)
    return jnp.take_along_axis(grid, (jnp.arange(top)[None, :] + turn) % top, axis=1)


def shares(count, total, bound, slope, full):
    loads = [(1 << 20) // math.isqrt(rank ** slope) + 1 for rank in range(1, count + 1)]
    largest = bound if full else min(bound, max(-(-total // count), total * loads[0] // sum(loads)))
    least = 1 if total - largest >= count - 1 else 0
    counts, spare = [largest] + [least] * (count - 1), total - largest - least * (count - 1)
    while spare > 0:
        candidates = [i for i in range(1, count) if counts[i] < largest] or [i for i in range(1, count) if counts[i] < bound]
        mass, remaining = sum([loads[i] for i in candidates]), spare
        for i in candidates:
            more = min(bound - counts[i], max(1, remaining * loads[i] // mass), spare)
            counts[i] = counts[i] + more
            spare = spare - more
    return np.array(counts)


def bell_draw(rng, shape, width, most, cuts=(), kind=jnp.bfloat16):
    loudness = levels(rng, shape, cuts, -0.22, 0.18) if cuts else 1.0
    entries = jax.random.normal(rng, shape, jnp.float32) * width * loudness
    return jnp.minimum(jnp.maximum(entries, -most), most).astype(kind)


def setup_inputs(seed: int = 0, part: int = 0) -> dict:
    arg_keys = jax.random.split(jax.random.key(seed), 10)
    own_keys = jax.random.split(jax.random.fold_in(arg_keys[9], part), 10)
    byte_rows = draw_byte_rows(jax.random.fold_in(jax.random.fold_in(arg_keys[9], part), 71), part)
    patch_lengths = jax.vmap(lambda own: ragged_sizes(own, PATCH_DEV, BYTE_DEV, MAXLEN, 2))(jax.random.split(own_keys[1], (N_SEQ * N_DP))).reshape((N_SEQ * N_DP, PATCH_DEV)).astype(jnp.int32)
    patch_owner_keys = jax.random.split(jax.random.fold_in(own_keys[2], 1), PATCHES // PATCH_DEV)
    patch_owner_turns = jax.random.permutation(jax.random.fold_in(own_keys[2], 3), PATCHES // PATCH_DEV)
    patch_owner = jax.vmap(lambda own, number: shared_out(jax.random.fold_in(own_keys[2], 2), own, number, PATCH_DEV, N_SEQ * N_DP, 1, CAP, 1))(patch_owner_keys, patch_owner_turns).reshape((PATCHES, 1))
    patch_stream = draw_patch_stream(jax.random.fold_in(jax.random.fold_in(arg_keys[9], part), 71), part)
    w_in = bell_draw(arg_keys[4], (DL, D), DL ** -0.5, 0.1875, ((0, 8), (1, 2)))
    norm_gain = jnp.clip(1.0 + 0.18 * jax.random.normal(arg_keys[5], (D,), jnp.float32), 0.1, 1.9)
    w_kv = bell_draw(arg_keys[6], (2, D, DL), D ** -0.5, 0.09375, ((1, 2), (2, 8)))
    w_query = bell_draw(arg_keys[7], (DL, DL), DL ** -0.5, 0.1875, ((1, 2),))
    w_out = bell_draw(arg_keys[8], (DL, DL), DL ** -0.5, 0.1875, ((1, 2),))
    return dict(byte_rows=byte_rows, patch_lengths=patch_lengths, patch_owner=patch_owner, patch_stream=patch_stream, w_in=w_in, norm_gain=norm_gain, w_kv=w_kv, w_query=w_query, w_out=w_out)


def pool_block(pair):
    rows, lens = pair
    ends = jnp.cumsum(lens)
    starts = ends - lens
    places = jnp.arange(rows.shape[0], dtype=jnp.int32)
    members = ((places[None, :] >= starts[:, None]) & (places[None, :] < ends[:, None])).astype(jnp.bfloat16)
    sums = jnp.dot(members, rows, preferred_element_type=jnp.float32)
    return (sums / lens[:, None].astype(jnp.float32)).astype(jnp.bfloat16)

def reference(byte_rows, patch_lengths, patch_owner, patch_stream, w_in, norm_gain, w_kv, w_query, w_out):
    blocks = N_SEQ * N_DP
    rows_blocks = byte_rows.reshape(blocks, BYTE_DEV, DL)
    pooled = lax.map(pool_block, (rows_blocks, patch_lengths)).reshape(PATCHES, DL)
    owners = patch_owner[:, 0].reshape(blocks, PATCH_DEV)
    match = (owners[:, :, None] == jnp.arange(blocks, dtype=jnp.int32)[None, None, :]).astype(jnp.int32)
    ranking = lax.optimization_barrier(jnp.sum(jnp.cumsum(match, axis=1) * match, axis=2)) - 1
    slot = owners * SLOTS + jnp.arange(blocks, dtype=jnp.int32)[:, None] * CAP + ranking
    stream = patch_stream[slot.reshape(-1)]
    mixed = stream.astype(jnp.float32) + jnp.dot(pooled, w_in, preferred_element_type=jnp.float32)
    normed = (mixed * lax.rsqrt(lax.optimization_barrier(jnp.mean(mixed * mixed, axis=1, keepdims=True)) + 1e-06) * norm_gain[None, :]).astype(jnp.bfloat16)
    keys = jnp.dot(normed, w_kv[0], preferred_element_type=jnp.float32).astype(jnp.bfloat16)
    values = jnp.dot(normed, w_kv[1], preferred_element_type=jnp.float32).astype(jnp.bfloat16)
    query = jnp.dot(byte_rows, w_query, preferred_element_type=jnp.float32).astype(jnp.bfloat16)
    padding = jnp.zeros((WIN - 1, DL), jnp.bfloat16)
    keys_padded = jnp.concatenate([padding, keys], axis=0)
    values_padded = jnp.concatenate([padding, values], axis=0)
    scale = 1.0 / math.sqrt(HEAD_DIM)
    heads = DL // HEAD_DIM

    def attend(triple):
        block_query, lens, index = triple
        ends = jnp.cumsum(lens)
        places = jnp.arange(BYTE_DEV, dtype=jnp.int32)
        mine = lax.optimization_barrier(jnp.sum((ends[None, :] <= places[:, None]).astype(jnp.int32), axis=1))
        start = (index * PATCH_DEV).astype(jnp.int32)
        block_keys = lax.dynamic_slice_in_dim(keys_padded, start, PATCH_DEV + WIN - 1, 0)
        block_values = lax.dynamic_slice_in_dim(values_padded, start, PATCH_DEV + WIN - 1, 0)
        key_index = jnp.arange(PATCH_DEV + WIN - 1, dtype=jnp.int32) - (WIN - 1)
        allowed = (key_index[None, :] <= mine[:, None]) & (key_index[None, :] > mine[:, None] - WIN)
        allowed = allowed & (key_index[None, :] + start >= 0)
        q = block_query.reshape(BYTE_DEV, heads, HEAD_DIM).astype(jnp.float32)
        k = block_keys.reshape(-1, heads, HEAD_DIM).astype(jnp.float32)
        v = block_values.reshape(-1, heads, HEAD_DIM).astype(jnp.float32)
        scores = jnp.einsum('ihe,khe->hik', q, k) * scale
        scores = jnp.where(allowed[None, :, :], scores, -1e+30)
        top = lax.optimization_barrier(jnp.max(scores, axis=-1, keepdims=True))
        expo = jnp.exp(scores - top)
        weights = (expo / lax.optimization_barrier(jnp.sum(expo, axis=-1, keepdims=True))).astype(jnp.bfloat16)
        out = jnp.einsum('hik,khe->ihe', weights.astype(jnp.float32), v)
        return out.astype(jnp.bfloat16).reshape(BYTE_DEV, DL)
    attended = lax.map(attend, (query.reshape(blocks, BYTE_DEV, DL), patch_lengths, jnp.arange(blocks, dtype=jnp.int32)))
    attended = attended.reshape(BYTES, DL)
    return (byte_rows.astype(jnp.float32) + jnp.dot(attended, w_out, preferred_element_type=jnp.float32)).astype(jnp.bfloat16)
```

```python
import functools
import math

import jax
import jax.numpy as jnp
from jax import lax
from jax.experimental import pallas as pl
from jax.experimental.pallas import tpu as pltpu
from jax.sharding import PartitionSpec as P

D = 4096
HEAD_DIM = 64
WIN = 8


def shifted(block, axis, distance):
    devices = range(lax.axis_size(axis))
    route = [(i - distance, i) for i in devices if i - distance in devices]
    return lax.ppermute(block, axis, route)


def local(
    byte_rows, patch_lengths, patch_owner, patch_stream, w_in, norm_gain, w_kv, w_query, w_out
):
    sources = lax.axis_size(("seq", "dp"))
    lens = patch_lengths[0]
    count = lens.shape[0]
    byte_count = byte_rows.shape[0]
    slots = patch_stream.shape[0]
    cap = slots // sources
    quarter = w_query.shape[1]
    ends = jnp.cumsum(lens)
    starts = ends - lens
    places = jnp.arange(byte_count, dtype=jnp.int32)
    members = ((places[None, :] >= starts[:, None]) & (places[None, :] < ends[:, None])).astype(
        jnp.bfloat16
    )
    sums = jnp.dot(members, byte_rows, preferred_element_type=jnp.float32)
    pooled = (sums / lens[:, None].astype(jnp.float32)).astype(jnp.bfloat16)
    owners = patch_owner[:, 0]
    match = (owners[:, None] == jnp.arange(sources, dtype=jnp.int32)[None, :]).astype(jnp.int32)
    ranking = jnp.sum(jnp.cumsum(match, axis=0) * match, axis=1) - 1
    targets = owners * cap + ranking
    dispatch = (jnp.arange(slots, dtype=jnp.int32)[:, None] == targets[None, :]).astype(
        jnp.bfloat16
    )
    outgoing = jnp.dot(dispatch, pooled, preferred_element_type=jnp.float32).astype(jnp.bfloat16)
    outgoing = outgoing.reshape(sources, cap, outgoing.shape[1])
    arrived = lax.all_to_all(outgoing, ("seq", "dp"), split_axis=0, concat_axis=0, tiled=True)
    inputs = arrived.reshape(slots, arrived.shape[2])
    mixed = jnp.dot(
        inputs,
        lax.all_gather(w_in, ("seq", "dp"), axis=0, tiled=True),
        preferred_element_type=jnp.float32,
    )
    mixed = mixed + patch_stream.astype(jnp.float32)
    squares = lax.psum(jnp.sum(mixed * mixed, axis=1), "tp")
    normed = (mixed * lax.rsqrt(squares / D + 1e-06)[:, None] * norm_gain[None, :]).astype(
        jnp.bfloat16
    )
    partial_kv = jnp.einsum(
        "sd,kdc->skc",
        normed,
        lax.all_gather(w_kv, ("seq", "dp"), axis=2, tiled=True),
        preferred_element_type=jnp.float32,
    )
    kv_slots = lax.psum_scatter(partial_kv, "tp", scatter_dimension=2, tiled=True).astype(
        jnp.bfloat16
    )
    returned = lax.all_to_all(
        kv_slots.reshape(sources, cap, 2, quarter),
        ("seq", "dp"),
        split_axis=0,
        concat_axis=0,
        tiled=True,
    )
    kv_patch = jnp.einsum(
        "sp,skc->pkc",
        dispatch,
        returned.reshape(slots, 2, quarter),
        preferred_element_type=jnp.float32,
    ).astype(jnp.bfloat16)
    prior = shifted(kv_patch[count - (WIN - 1) :], ("seq", "dp"), 1)
    window_kv = jnp.concatenate([prior, kv_patch], axis=0)
    query = jnp.dot(byte_rows, w_query, preferred_element_type=jnp.float32).astype(jnp.bfloat16)
    heads = quarter // HEAD_DIM
    mine = jnp.sum((ends[None, :] <= places[:, None]).astype(jnp.int32), axis=1)
    key_index = jnp.arange(count + WIN - 1, dtype=jnp.int32) - (WIN - 1)
    first_block = lax.axis_index(("seq", "dp")) == 0
    allowed = (key_index[None, :] <= mine[:, None]) & (key_index[None, :] > mine[:, None] - WIN)
    allowed = allowed & ((key_index[None, :] >= 0) | jnp.logical_not(first_block))
    queries = query.reshape(byte_count, heads, HEAD_DIM)
    keys = window_kv[:, 0].reshape(-1, heads, HEAD_DIM)
    values = window_kv[:, 1].reshape(-1, heads, HEAD_DIM)
    scores = jnp.einsum("ihe,khe->hik", queries, keys, preferred_element_type=jnp.float32) * (
        1.0 / math.sqrt(HEAD_DIM)
    )
    scores = jnp.where(allowed[None, :, :], scores, -1e30)
    top = jnp.max(scores, axis=-1, keepdims=True)
    expo = jnp.exp(scores - top)
    weights = (expo / jnp.sum(expo, axis=-1, keepdims=True)).astype(jnp.bfloat16)
    attended = jnp.einsum("hik,khe->ihe", weights, values, preferred_element_type=jnp.float32)
    attended = attended.astype(jnp.bfloat16).reshape(byte_count, quarter)
    projected = jnp.dot(
        lax.all_gather(attended, "tp", axis=1, tiled=True),
        w_out,
        preferred_element_type=jnp.float32,
    )
    residual = lax.dynamic_slice_in_dim(byte_rows, lax.axis_index("tp") * quarter, quarter, 1)
    return (residual.astype(jnp.float32) + projected).astype(jnp.bfloat16)


MESH = pl.DeviceIdType.MESH
HALO = 16
ROWS = 128
bf16, f32 = jnp.bfloat16, jnp.float32


def iota(shape, axis):
    return lax.broadcasted_iota(jnp.int32, shape, axis)


def fused_kernel(
    n_seq,
    rows_ref, lens_ref, own_col_ref, own_row_ref, stream_ref, w_in_ref, gain_ref, w_kv_ref,
    w_query_ref, w_out_ref, out_ref,
    win, wkv, arr, br, wq, wo, pooled, mixed, nrm, hs_out, hs_in, part, part_out, part_in,
    kv, sq, sq_in, query, att, y_out,
    recv, send_r, send_l, send_y, send_c, local_sem, st_send, st_recv, x_send, x_recv,
    xc_send, xc_recv, h_send, h_recv, p_send, p_recv, y_send, y_recv,
):
    g, s = lax.axis_index("groups"), lax.axis_index("seq")
    t, d = lax.axis_index("tp"), lax.axis_index("dp")
    n = n_seq * 2
    me = s * 2 + d
    count = own_col_ref.shape[0]
    byte_count, dl = rows_ref.shape
    half = byte_count // 2
    depth, width = w_in_ref.shape
    cap = stream_ref.shape[0] // n
    cols = w_query_ref.shape[1]
    hd = depth // 2
    hw = width // 2
    y_peer, c_peer, x_peer = {"groups": 1 - g}, {"dp": 1 - d}, {"tp": 1 - t}

    barrier = pltpu.get_barrier_semaphore()

    def other(i):
        b = lax.rem(me + i, n)
        return b, {"seq": b // 2, "dp": lax.rem(b, 2)}

    for i in range(1, n):
        pl.semaphore_signal(barrier, inc=1, device_id=other(i)[1], device_id_type=MESH)
    pl.semaphore_signal(barrier, inc=1, device_id=y_peer, device_id_type=MESH)
    pl.semaphore_signal(barrier, inc=1, device_id=x_peer, device_id_type=MESH)

    local = []

    def bring(src, dst):
        copy = pltpu.make_async_copy(src, dst, local_sem.at[len(local)])
        copy.start()
        local.append(copy)

    bring(rows_ref, br)
    bring(stream_ref.at[pl.ds(pl.multiple_of(me * cap, cap), cap)], arr.at[pl.ds(pl.multiple_of(me * cap, cap), cap)])
    bring(w_query_ref, wq.at[t])
    bring(w_out_ref, wo.at[t])
    bring(w_in_ref, win.at[pl.ds(pl.multiple_of(me * depth, depth), depth)])
    bring(w_kv_ref, wkv.at[me])
    pl.semaphore_wait(barrier, n + 1)

    def remote(src, dst, send, arrive, where):
        return pltpu.make_async_remote_copy(
            src_ref=src, dst_ref=dst, send_sem=send, recv_sem=arrive, device_id=where, device_id_type=MESH
        )

    def held(kind, slot, h):
        if kind == 0:
            return win.at[pl.ds(pl.multiple_of(slot * depth + h * hd, hd), hd)]
        return wkv.at[slot, h, pl.ds((kind - 1) * hw, hw)]

    def own(kind, h):
        if kind == 0:
            return w_in_ref.at[pl.ds(pl.multiple_of(h * hd, hd), hd)]
        return w_kv_ref.at[h, pl.ds((kind - 1) * hw, hw)]

    def piece(kind, z, h, send, where, mine=False, core=None):
        slot = z * 2 + (d if core is None else core)
        dst = held(kind, slot, h)
        return remote(own(kind, h) if mine else dst, dst, send, recv.at[kind, slot, h], where)

    def right(kind, z, mine=False):
        return piece(kind, z, g, send_r.at[kind, z], {"seq": jnp.minimum(s + 1, n_seq - 1)}, mine)

    def left(kind, z, mine=False):
        return piece(kind, z, g, send_l.at[kind, z], {"seq": jnp.maximum(s - 1, 0)}, mine)

    def across(kind, z):
        return piece(kind, z, g, send_y.at[kind, z], y_peer)

    def core(kind, z, h, mine=False):
        return piece(kind, z, h, send_c.at[kind, z, h], c_peer, mine)

    def ends_of_line(kind):
        pl.when(s + 1 < n_seq)(lambda: right(kind, s, True).start())
        pl.when(s > 0)(lambda: left(kind, s, True).start())

    def each(k, fn):
        pl.when(s - k >= 0)(lambda: fn(s - k, True))
        pl.when(s + k < n_seq)(lambda: fn(s + k, False))

    def arrive(kind, k):
        def one(z, from_left):
            piece(kind, z, g, send_y.at[kind, z], y_peer).wait_recv()
            if from_left:
                pl.when(s + 1 < n_seq)(lambda: right(kind, z).start())
            else:
                pl.when(s > 0)(lambda: left(kind, z).start())
            across(kind, z).start()
            core(kind, z, g).start()
        each(k, one)

    def arrive_y(kind, k):
        def one(z, _):
            piece(kind, z, 1 - g, send_y.at[kind, z], y_peer).wait_recv()
            core(kind, z, 1 - g).start()
        each(k, one)

    def arrive_c(kind, k):
        def one(z, _=None):
            for h in range(2):
                piece(kind, z, h, send_c.at[kind, z, h], c_peer, core=1 - d).wait_recv()
        one(s) if k == 0 else each(k, one)

    ends_of_line(0)

    def stream_copy(i):
        b, where = other(i)
        src = stream_ref.at[pl.ds(pl.multiple_of(b * cap, cap), cap)]
        dst = arr.at[pl.ds(pl.multiple_of(me * cap, cap), cap)]
        return remote(src, dst, st_send.at[i], st_recv.at[i], where)

    for i in range(1, n):
        stream_copy(i).start()
    dh = dl // 2
    mine_rows = pl.ds(pl.multiple_of(d * dh, dh), dh)

    def x_copy(i):
        src, dst = ((w_query_ref, wq), (w_out_ref, wo))[i]
        return remote(src.at[mine_rows], dst.at[t, mine_rows], x_send.at[i], x_recv.at[i], x_peer)

    def xc_copy(i):
        dst = (wq, wo)[i].at[1 - t, mine_rows]
        return remote(dst, dst, xc_send.at[i], xc_recv.at[i], c_peer)

    x_copy(0).start()
    x_copy(1).start()
    for kind in range(3):
        for h in range(2):
            core(kind, s, h, True).start()
    ends_of_line(1)
    ends_of_line(2)

    local[0].wait()
    lens_row = lens_ref[...]
    tri = iota((count, count), 1) <= iota((count, count), 0)
    ends_col = jnp.sum(jnp.where(tri, lens_row, 0).astype(f32), axis=1, keepdims=True)
    lens_col = jnp.sum(
        jnp.where(iota((count, count), 0) == iota((count, count), 1), lens_row, 0).astype(f32), axis=1, keepdims=True
    )
    places = iota((count, byte_count), 1).astype(f32)
    members = jnp.where((places >= ends_col - lens_col) & (places < ends_col), 1.0, 0.0).astype(bf16)
    sums = jnp.dot(members, br[...], preferred_element_type=f32)
    pooled[pl.ds(0, count)] = (sums / lens_col).astype(bf16)
    _, following = other(1)
    halo_pooled = remote(
        pooled.at[pl.ds(count - HALO, HALO)], pooled.at[pl.ds(count, HALO)], h_send.at[0], h_recv.at[0], following
    )
    halo_pooled.start()

    arrive(0, 1)
    x_copy(0).wait_recv()
    xc_copy(0).start()
    x_copy(1).wait_recv()
    xc_copy(1).start()
    arrive(0, 2)
    local[2].wait()
    xc_copy(0).wait_recv()
    my_bytes = pl.ds(pl.multiple_of(t * half, half), half)
    for part_t in range(2):
        query[:, part_t * cols:(part_t + 1) * cols] = jnp.dot(
            br[my_bytes, :], wq[part_t], preferred_element_type=f32
        ).astype(bf16)
    arrive_y(0, 1)
    arrive(0, 3)

    for i in range(1, n):
        stream_copy(i).wait_recv()
    local[1].wait()
    owner = own_col_ref[...]
    same = (owner == own_row_ref[...]) & (iota((count, count), 1) < iota((count, count), 0))
    ranking = jnp.sum(jnp.where(same, 1.0, 0.0), axis=1, keepdims=True)
    target = owner.astype(f32) * cap + ranking
    pick = jnp.where(iota((count, n * cap), 1).astype(f32) == target, 1.0, 0.0).astype(bf16)
    mixed[pl.ds(0, count)] = jnp.dot(pick, arr[...], preferred_element_type=f32)
    hs_out[...] = mixed[pl.ds(count - HALO, HALO)].astype(bf16)
    halo_stream = remote(hs_out, hs_in, h_send.at[1], h_recv.at[1], following)
    halo_stream.start()
    arrive(1, 1)
    arrive_y(0, 2)
    arrive(2, 1)
    arrive_y(0, 3)
    for k in range(n_seq):
        arrive_c(0, k)
    local[4].wait()
    halo_pooled.wait_recv()
    halo_stream.wait_recv()
    mixed[pl.ds(count, HALO)] = hs_in[...].astype(f32)
    step = 512
    total = jnp.zeros((count + HALO, 128), f32)
    for c in range(width // step):
        at = pl.ds(c * step, step)
        now = mixed[:, at] + jnp.dot(pooled[...], win[:, at], preferred_element_type=f32)
        nrm[:, at] = (now * gain_ref[:, at]).astype(bf16)
        for j in range(step // 128):
            lane = now[:, j * 128:(j + 1) * 128]
            total = total + lane * lane
    sq[...] = total
    sq_copy = remote(sq, sq_in, p_send.at[n], p_recv.at[n], x_peer)
    sq_copy.start()

    def part_copy(slot):
        return remote(part_out.at[slot], part_in.at[slot], p_send.at[slot], p_recv.at[slot], x_peer)

    def project(z, _=None):
        for c in range(2):
            slot = z * 2 + c
            for h in range(2):
                val = jnp.dot(nrm[...], wkv[slot, h], preferred_element_type=f32)
                part[slot, :, pl.ds(h * 128, 128)] = val
                part_out[slot, :, pl.ds(h * 128, 128)] = val.astype(bf16)
            part_copy(slot).start()

    arrive(1, 2)
    arrive_y(1, 1)
    arrive(2, 2)
    arrive_y(2, 1)
    local[5].wait()
    arrive_c(1, 0)
    arrive_c(2, 0)
    project(s)
    arrive(1, 3)
    arrive_y(1, 2)
    arrive(2, 3)
    arrive_c(1, 1)
    arrive_c(2, 1)
    each(1, project)
    arrive_y(2, 2)
    arrive_y(1, 3)
    arrive_c(1, 2)
    arrive_c(2, 2)
    each(2, project)
    arrive_y(2, 3)
    arrive_c(1, 3)
    arrive_c(2, 3)
    each(3, project)

    ends_row = jnp.dot(
        jnp.broadcast_to(lens_row.astype(f32), (8, count)).astype(bf16),
        jnp.where(iota((count, count), 0) <= iota((count, count), 1), 1.0, 0.0).astype(bf16),
        preferred_element_type=f32,
    )[0:1]
    sq_copy.wait_recv()
    square = jnp.sum(sq[...] + sq_in[...], axis=1, keepdims=True)
    scale = lax.rsqrt(square / D + 1e-06)

    def finish(slot, carry):
        part_copy(slot).wait_recv()
        kv[slot] = ((part[slot] + part_in[slot].astype(f32)) * scale).astype(bf16)
        return carry

    lax.fori_loop(0, n, finish, 0)
    local[3].wait()
    xc_copy(1).wait_recv()
    keys_n = count + HALO
    key = iota((1, keys_n), 1)
    key = jnp.where(key < count, key, key - keys_n).astype(f32)
    first = me == 0
    low_half = iota((keys_n, 128), 1) < HEAD_DIM

    def y_copy(r):
        at = pl.ds(pl.multiple_of(t * half + r * ROWS, ROWS), ROWS)
        return remote(y_out.at[pl.ds(r * ROWS, ROWS)], out_ref.at[at], y_send.at[r], y_recv.at[r], x_peer)

    for r in range(half // ROWS):
        place = (iota((ROWS, 1), 0) + (t * half + r * ROWS)).astype(f32)
        patch = jnp.sum(jnp.where(ends_row <= place, 1.0, 0.0), axis=1, keepdims=True)
        floor = jnp.where(first, jnp.maximum(patch - WIN, -1.0), patch - WIN)
        bias = jnp.where((key <= patch) & (key > floor), 0.0, -1e30)

        def heads(slot, carry):
            at = pl.ds(pl.multiple_of(slot * 128, 128), 128)
            q = query[pl.ds(r * ROWS, ROWS), at]
            keys, values = kv[slot, :, pl.ds(0, 128)], kv[slot, :, pl.ds(128, 128)]
            result = jnp.zeros((ROWS, 128), f32)
            for low in (True, False):
                pick_head = low_half if low else jnp.logical_not(low_half)
                kh = jnp.where(pick_head, keys, jnp.zeros_like(keys))
                vh = jnp.where(pick_head, values, jnp.zeros_like(values))
                scores = lax.dot_general(q, kh, (((1,), (1,)), ((), ())), preferred_element_type=f32)
                scores = scores * (1.0 / math.sqrt(HEAD_DIM)) + bias
                expo = jnp.exp(scores - jnp.max(scores, axis=1, keepdims=True))
                weights = (expo / jnp.sum(expo, axis=1, keepdims=True)).astype(bf16)
                result = result + jnp.dot(weights, vh, preferred_element_type=f32)
            att[pl.ds(r * ROWS, ROWS), at] = result.astype(bf16)
            return carry

        lax.fori_loop(0, n, heads, 0)
        at = pl.ds(pl.multiple_of(t * half + r * ROWS, ROWS), ROWS)
        a = att[pl.ds(r * ROWS, ROWS), :]
        for who in (1 - t, t):
            at_cols = pl.ds(pl.multiple_of(who * cols, cols), cols)
            value = br[at, at_cols].astype(f32) + jnp.dot(a, wo[who], preferred_element_type=f32)
            if who is t:
                out_ref[at, :] = value.astype(bf16)
            else:
                y_out[pl.ds(r * ROWS, ROWS), :] = value.astype(bf16)
                y_copy(r).start()

    for r in range(half // ROWS):
        y_copy(r).wait()
    for kind in range(3):
        pl.when(s + 1 < n_seq)(lambda: right(kind, s, True).wait_send())
        pl.when(s > 0)(lambda: left(kind, s, True).wait_send())
        for h in range(2):
            core(kind, s, h, True).wait_send()
        for k in range(1, n_seq):
            def sent(z, from_left):
                if from_left:
                    pl.when(s + 1 < n_seq)(lambda: right(kind, z).wait_send())
                else:
                    pl.when(s > 0)(lambda: left(kind, z).wait_send())
                across(kind, z).wait_send()
                core(kind, z, 0).wait_send()
                core(kind, z, 1).wait_send()
            each(k, sent)
    for i in range(1, n):
        stream_copy(i).wait_send()
    for i in range(2):
        x_copy(i).wait_send()
        xc_copy(i).wait_send()
    halo_pooled.wait_send()
    halo_stream.wait_send()
    sq_copy.wait_send()
    lax.fori_loop(0, n, lambda slot, carry: (part_copy(slot).wait_send(), carry)[1], 0)


def fused(
    byte_rows, patch_lengths, patch_owner, patch_stream, w_in, norm_gain, w_kv, w_query, w_out
):
    n_seq = lax.axis_size("seq")
    n = n_seq * 2
    byte_count, dl = byte_rows.shape
    count = patch_owner.shape[0]
    depth, width = w_in.shape
    cols = w_query.shape[1]
    half = byte_count // 2
    tall = count + HALO
    chunks = half // ROWS
    any_spec, vmem = pl.BlockSpec(memory_space=pl.ANY), pl.BlockSpec(memory_space=pltpu.VMEM)
    dma = pltpu.SemaphoreType.DMA
    return pl.pallas_call(
        functools.partial(fused_kernel, n_seq),
        out_shape=jax.ShapeDtypeStruct((byte_count, cols), bf16),
        in_specs=[any_spec, vmem, vmem, vmem, any_spec, any_spec, vmem, any_spec, any_spec, any_spec],
        out_specs=vmem,
        scratch_shapes=[
            pltpu.VMEM((n * depth, width), bf16),
            pltpu.VMEM((n, 2, width, 128), bf16),
            pltpu.VMEM(patch_stream.shape, bf16),
            pltpu.VMEM((byte_count, dl), bf16),
            pltpu.VMEM((2, dl, cols), bf16),
            pltpu.VMEM((2, dl, cols), bf16),
            pltpu.VMEM((tall, dl), bf16),
            pltpu.VMEM((tall, width), f32),
            pltpu.VMEM((tall, width), bf16),
            pltpu.VMEM((HALO, width), bf16),
            pltpu.VMEM((HALO, width), bf16),
            pltpu.VMEM((n, tall, 256), f32),
            pltpu.VMEM((n, tall, 256), bf16),
            pltpu.VMEM((n, tall, 256), bf16),
            pltpu.VMEM((n, tall, 256), bf16),
            pltpu.VMEM((tall, 128), f32),
            pltpu.VMEM((tall, 128), f32),
            pltpu.VMEM((half, dl), bf16),
            pltpu.VMEM((half, dl), bf16),
            pltpu.VMEM((half, cols), bf16),
            dma((3, n, 2)),
            dma((3, n_seq)),
            dma((3, n_seq)),
            dma((3, n_seq)),
            dma((3, n_seq, 2)),
            dma((6,)),
            dma((n,)),
            dma((n,)),
            dma((2,)),
            dma((2,)),
            dma((2,)),
            dma((2,)),
            dma((2,)),
            dma((2,)),
            dma((n + 1,)),
            dma((n + 1,)),
            dma((chunks,)),
            dma((chunks,)),
        ],
        compiler_params=pltpu.CompilerParams(
            collective_id=0, has_side_effects=True, vmem_limit_bytes=56 * 1024 * 1024
        ),
        cost_estimate=pl.CostEstimate(flops=9 * 10**9, bytes_accessed=8 * 10**6, transcendentals=2 * 10**6),
    )(
        byte_rows, patch_lengths, patch_owner, patch_owner.reshape(1, count), patch_stream, w_in,
        norm_gain.reshape(1, width), w_kv, w_query, w_out,
    )


def solution(mesh):
    sizes = mesh.shape
    fits = sizes["groups"] == 2 and sizes["tp"] == 2 and sizes["dp"] == 2 and sizes["seq"] == 4
    return jax.shard_map(
        fused if fits else local,
        mesh=mesh,
        in_specs=(
            P(("groups", "seq", "dp"), None),
            P(("groups", "seq", "dp"), None),
            P(("groups", "seq", "dp"), None),
            P(("groups", "seq", "dp"), "tp"),
            P(("seq", "dp"), "tp"),
            P("tp"),
            P(None, "tp", ("seq", "dp")),
            P(None, "tp"),
            P(None, "tp"),
        ),
        out_specs=P(("groups", "seq", "dp"), "tp"),
        check_vma=False,
    )
```

```python
import functools
import math

import jax
import jax.numpy as jnp
from jax import lax
from jax.experimental import pallas as pl
from jax.experimental.pallas import tpu as pltpu
from jax.sharding import PartitionSpec as P

D = 4096
HEAD_DIM = 64
WIN = 8


def shifted(block, axis, distance):
    devices = range(lax.axis_size(axis))
    route = [(i - distance, i) for i in devices if i - distance in devices]
    return lax.ppermute(block, axis, route)


def local(
    byte_rows, patch_lengths, patch_owner, patch_stream, w_in, norm_gain, w_kv, w_query, w_out
):
    sources = lax.axis_size(("seq", "dp"))
    lens = patch_lengths[0]
    count = lens.shape[0]
    byte_count = byte_rows.shape[0]
    slots = patch_stream.shape[0]
    cap = slots // sources
    quarter = w_query.shape[1]
    ends = jnp.cumsum(lens)
    starts = ends - lens
    places = jnp.arange(byte_count, dtype=jnp.int32)
    members = ((places[None, :] >= starts[:, None]) & (places[None, :] < ends[:, None])).astype(
        jnp.bfloat16
    )
    sums = jnp.dot(members, byte_rows, preferred_element_type=jnp.float32)
    pooled = (sums / lens[:, None].astype(jnp.float32)).astype(jnp.bfloat16)
    owners = patch_owner[:, 0]
    match = (owners[:, None] == jnp.arange(sources, dtype=jnp.int32)[None, :]).astype(jnp.int32)
    ranking = jnp.sum(jnp.cumsum(match, axis=0) * match, axis=1) - 1
    targets = owners * cap + ranking
    dispatch = (jnp.arange(slots, dtype=jnp.int32)[:, None] == targets[None, :]).astype(
        jnp.bfloat16
    )
    outgoing = jnp.dot(dispatch, pooled, preferred_element_type=jnp.float32).astype(jnp.bfloat16)
    outgoing = outgoing.reshape(sources, cap, outgoing.shape[1])
    arrived = lax.all_to_all(outgoing, ("seq", "dp"), split_axis=0, concat_axis=0, tiled=True)
    inputs = arrived.reshape(slots, arrived.shape[2])
    mixed = jnp.dot(
        inputs,
        lax.all_gather(w_in, ("seq", "dp"), axis=0, tiled=True),
        preferred_element_type=jnp.float32,
    )
    mixed = mixed + patch_stream.astype(jnp.float32)
    squares = lax.psum(jnp.sum(mixed * mixed, axis=1), "tp")
    normed = (mixed * lax.rsqrt(squares / D + 1e-06)[:, None] * norm_gain[None, :]).astype(
        jnp.bfloat16
    )
    partial_kv = jnp.einsum(
        "sd,kdc->skc",
        normed,
        lax.all_gather(w_kv, ("seq", "dp"), axis=2, tiled=True),
        preferred_element_type=jnp.float32,
    )
    kv_slots = lax.psum_scatter(partial_kv, "tp", scatter_dimension=2, tiled=True).astype(
        jnp.bfloat16
    )
    returned = lax.all_to_all(
        kv_slots.reshape(sources, cap, 2, quarter),
        ("seq", "dp"),
        split_axis=0,
        concat_axis=0,
        tiled=True,
    )
    kv_patch = jnp.einsum(
        "sp,skc->pkc",
        dispatch,
        returned.reshape(slots, 2, quarter),
        preferred_element_type=jnp.float32,
    ).astype(jnp.bfloat16)
    prior = shifted(kv_patch[count - (WIN - 1) :], ("seq", "dp"), 1)
    window_kv = jnp.concatenate([prior, kv_patch], axis=0)
    query = jnp.dot(byte_rows, w_query, preferred_element_type=jnp.float32).astype(jnp.bfloat16)
    heads = quarter // HEAD_DIM
    mine = jnp.sum((ends[None, :] <= places[:, None]).astype(jnp.int32), axis=1)
    key_index = jnp.arange(count + WIN - 1, dtype=jnp.int32) - (WIN - 1)
    first_block = lax.axis_index(("seq", "dp")) == 0
    allowed = (key_index[None, :] <= mine[:, None]) & (key_index[None, :] > mine[:, None] - WIN)
    allowed = allowed & ((key_index[None, :] >= 0) | jnp.logical_not(first_block))
    queries = query.reshape(byte_count, heads, HEAD_DIM)
    keys = window_kv[:, 0].reshape(-1, heads, HEAD_DIM)
    values = window_kv[:, 1].reshape(-1, heads, HEAD_DIM)
    scores = jnp.einsum("ihe,khe->hik", queries, keys, preferred_element_type=jnp.float32) * (
        1.0 / math.sqrt(HEAD_DIM)
    )
    scores = jnp.where(allowed[None, :, :], scores, -1e30)
    top = jnp.max(scores, axis=-1, keepdims=True)
    expo = jnp.exp(scores - top)
    weights = (expo / jnp.sum(expo, axis=-1, keepdims=True)).astype(jnp.bfloat16)
    attended = jnp.einsum("hik,khe->ihe", weights, values, preferred_element_type=jnp.float32)
    attended = attended.astype(jnp.bfloat16).reshape(byte_count, quarter)
    projected = jnp.dot(
        lax.all_gather(attended, "tp", axis=1, tiled=True),
        w_out,
        preferred_element_type=jnp.float32,
    )
    residual = lax.dynamic_slice_in_dim(byte_rows, lax.axis_index("tp") * quarter, quarter, 1)
    return (residual.astype(jnp.float32) + projected).astype(jnp.bfloat16)


MESH = pl.DeviceIdType.MESH
HALO = 16
ROWS = 128
bf16, f32 = jnp.bfloat16, jnp.float32


def iota(shape, axis):
    return lax.broadcasted_iota(jnp.int32, shape, axis)


def fused_kernel(
    n_seq,
    rows_ref, lens_ref, own_col_ref, own_row_ref, stream_ref, w_in_ref, gain_ref, w_kv_ref,
    w_query_ref, w_out_ref, out_ref,
    win, wkv, arr, br, wq, wo, pooled, mixed, nrm, hs_out, hs_in, part, part_out, part_in,
    kv, sq, sq_in, query, att, y_out,
    recv, send_r, send_l, send_y, send_c, local_sem, st_send, st_recv, x_send, x_recv,
    xc_send, xc_recv, h_send, h_recv, p_send, p_recv, y_send, y_recv,
):
    g, s = lax.axis_index("groups"), lax.axis_index("seq")
    t, d = lax.axis_index("tp"), lax.axis_index("dp")
    n = n_seq * 2
    me = s * 2 + d
    count = own_col_ref.shape[0]
    byte_count, dl = rows_ref.shape
    half = byte_count // 2
    depth, width = w_in_ref.shape
    cap = stream_ref.shape[0] // n
    cols = w_query_ref.shape[1]
    hd = depth // 2
    hw = width // 2
    y_peer, c_peer, x_peer = {"groups": 1 - g}, {"dp": 1 - d}, {"tp": 1 - t}

    barrier = pltpu.get_barrier_semaphore()

    def other(i):
        b = lax.rem(me + i, n)
        return b, {"seq": b // 2, "dp": lax.rem(b, 2)}

    for i in range(1, n):
        pl.semaphore_signal(barrier, inc=1, device_id=other(i)[1], device_id_type=MESH)
    pl.semaphore_signal(barrier, inc=1, device_id=y_peer, device_id_type=MESH)
    pl.semaphore_signal(barrier, inc=1, device_id=x_peer, device_id_type=MESH)

    local = []

    def bring(src, dst):
        copy = pltpu.make_async_copy(src, dst, local_sem.at[len(local)])
        copy.start()
        local.append(copy)

    bring(rows_ref, br)
    bring(stream_ref.at[pl.ds(pl.multiple_of(me * cap, cap), cap)], arr.at[pl.ds(pl.multiple_of(me * cap, cap), cap)])
    bring(w_query_ref, wq.at[t])
    bring(w_out_ref, wo.at[t])
    bring(w_in_ref, win.at[pl.ds(pl.multiple_of(me * depth, depth), depth)])
    bring(w_kv_ref, wkv.at[me])
    pl.semaphore_wait(barrier, n + 1)

    def remote(src, dst, send, arrive, where):
        return pltpu.make_async_remote_copy(
            src_ref=src, dst_ref=dst, send_sem=send, recv_sem=arrive, device_id=where, device_id_type=MESH
        )

    def held(kind, slot, h):
        if kind == 0:
            return win.at[pl.ds(pl.multiple_of(slot * depth + h * hd, hd), hd)]
        return wkv.at[slot, h, pl.ds((kind - 1) * hw, hw)]

    def own(kind, h):
        if kind == 0:
            return w_in_ref.at[pl.ds(pl.multiple_of(h * hd, hd), hd)]
        return w_kv_ref.at[h, pl.ds((kind - 1) * hw, hw)]

    def piece(kind, z, h, send, where, mine=False, core=None):
        slot = z * 2 + (d if core is None else core)
        dst = held(kind, slot, h)
        return remote(own(kind, h) if mine else dst, dst, send, recv.at[kind, slot, h], where)

    def right(kind, z, mine=False):
        return piece(kind, z, g, send_r.at[kind, z], {"seq": jnp.minimum(s + 1, n_seq - 1)}, mine)

    def left(kind, z, mine=False):
        return piece(kind, z, g, send_l.at[kind, z], {"seq": jnp.maximum(s - 1, 0)}, mine)

    def across(kind, z):
        return piece(kind, z, g, send_y.at[kind, z], y_peer)

    def core(kind, z, h, mine=False):
        return piece(kind, z, h, send_c.at[kind, z, h], c_peer, mine)

    def ends_of_line(kind):
        pl.when(s + 1 < n_seq)(lambda: right(kind, s, True).start())
        pl.when(s > 0)(lambda: left(kind, s, True).start())

    def each(k, fn):
        pl.when(s - k >= 0)(lambda: fn(s - k, True))
        pl.when(s + k < n_seq)(lambda: fn(s + k, False))

    def arrive(kind, k):
        def one(z, from_left):
            piece(kind, z, g, send_y.at[kind, z], y_peer).wait_recv()
            if from_left:
                pl.when(s + 1 < n_seq)(lambda: right(kind, z).start())
            else:
                pl.when(s > 0)(lambda: left(kind, z).start())
            across(kind, z).start()
            core(kind, z, g).start()
        each(k, one)

    def arrive_y(kind, k):
        def one(z, _):
            piece(kind, z, 1 - g, send_y.at[kind, z], y_peer).wait_recv()
            core(kind, z, 1 - g).start()
        each(k, one)

    def arrive_c(kind, k):
        def one(z, _=None):
            for h in range(2):
                piece(kind, z, h, send_c.at[kind, z, h], c_peer, core=1 - d).wait_recv()
        one(s) if k == 0 else each(k, one)

    ends_of_line(0)

    def stream_copy(i):
        b, where = other(i)
        src = stream_ref.at[pl.ds(pl.multiple_of(b * cap, cap), cap)]
        dst = arr.at[pl.ds(pl.multiple_of(me * cap, cap), cap)]
        return remote(src, dst, st_send.at[i], st_recv.at[i], where)

    for i in range(1, n):
        stream_copy(i).start()
    dh = dl // 2
    mine_rows = pl.ds(pl.multiple_of(d * dh, dh), dh)

    def x_copy(i):
        src, dst = ((w_query_ref, wq), (w_out_ref, wo))[i]
        return remote(src.at[mine_rows], dst.at[t, mine_rows], x_send.at[i], x_recv.at[i], x_peer)

    def xc_copy(i):
        dst = (wq, wo)[i].at[1 - t, mine_rows]
        return remote(dst, dst, xc_send.at[i], xc_recv.at[i], c_peer)

    x_copy(0).start()
    x_copy(1).start()
    for kind in range(3):
        for h in range(2):
            core(kind, s, h, True).start()
    ends_of_line(1)
    ends_of_line(2)

    local[0].wait()
    lens_row = lens_ref[...]
    tri = iota((count, count), 1) <= iota((count, count), 0)
    ends_col = jnp.sum(jnp.where(tri, lens_row, 0).astype(f32), axis=1, keepdims=True)
    lens_col = jnp.sum(
        jnp.where(iota((count, count), 0) == iota((count, count), 1), lens_row, 0).astype(f32), axis=1, keepdims=True
    )
    places = iota((count, byte_count), 1).astype(f32)
    members = jnp.where((places >= ends_col - lens_col) & (places < ends_col), 1.0, 0.0).astype(bf16)
    sums = jnp.dot(members, br[...], preferred_element_type=f32)
    pooled[pl.ds(0, count)] = (sums / lens_col).astype(bf16)
    _, following = other(1)
    halo_pooled = remote(
        pooled.at[pl.ds(count - HALO, HALO)], pooled.at[pl.ds(count, HALO)], h_send.at[0], h_recv.at[0], following
    )
    halo_pooled.start()

    arrive(0, 1)
    arrive(1, 1)
    x_copy(0).wait_recv()
    xc_copy(0).start()
    x_copy(1).wait_recv()
    xc_copy(1).start()
    arrive(2, 1)
    arrive_y(0, 1)
    arrive(0, 2)
    local[2].wait()
    xc_copy(0).wait_recv()
    my_bytes = pl.ds(pl.multiple_of(t * half, half), half)
    for part_t in range(2):
        query[:, part_t * cols:(part_t + 1) * cols] = jnp.dot(
            br[my_bytes, :], wq[part_t], preferred_element_type=f32
        ).astype(bf16)
    arrive_y(1, 1)
    arrive(1, 2)
    arrive_y(2, 1)
    arrive(2, 2)
    arrive_y(0, 2)
    arrive(0, 3)

    for i in range(1, n):
        stream_copy(i).wait_recv()
    local[1].wait()
    owner = own_col_ref[...]
    same = (owner == own_row_ref[...]) & (iota((count, count), 1) < iota((count, count), 0))
    ranking = jnp.sum(jnp.where(same, 1.0, 0.0), axis=1, keepdims=True)
    target = owner.astype(f32) * cap + ranking
    pick = jnp.where(iota((count, n * cap), 1).astype(f32) == target, 1.0, 0.0).astype(bf16)
    mixed[pl.ds(0, count)] = jnp.dot(pick, arr[...], preferred_element_type=f32)
    hs_out[...] = mixed[pl.ds(count - HALO, HALO)].astype(bf16)
    halo_stream = remote(hs_out, hs_in, h_send.at[1], h_recv.at[1], following)
    halo_stream.start()
    arrive_y(1, 2)
    arrive_y(0, 3)
    for k in range(n_seq):
        arrive_c(0, k)
    local[4].wait()
    halo_pooled.wait_recv()
    halo_stream.wait_recv()
    mixed[pl.ds(count, HALO)] = hs_in[...].astype(f32)
    step = 512
    total = jnp.zeros((count + HALO, 128), f32)
    for c in range(width // step):
        at = pl.ds(c * step, step)
        now = mixed[:, at] + jnp.dot(pooled[...], win[:, at], preferred_element_type=f32)
        nrm[:, at] = (now * gain_ref[:, at]).astype(bf16)
        for j in range(step // 128):
            lane = now[:, j * 128:(j + 1) * 128]
            total = total + lane * lane
    sq[...] = total
    sq_copy = remote(sq, sq_in, p_send.at[n], p_recv.at[n], x_peer)
    sq_copy.start()

    def part_copy(slot):
        return remote(part_out.at[slot], part_in.at[slot], p_send.at[slot], p_recv.at[slot], x_peer)

    def project(z, _=None):
        for c in range(2):
            slot = z * 2 + c
            for h in range(2):
                val = jnp.dot(nrm[...], wkv[slot, h], preferred_element_type=f32)
                part[slot, :, pl.ds(h * 128, 128)] = val
                part_out[slot, :, pl.ds(h * 128, 128)] = val.astype(bf16)
            part_copy(slot).start()

    arrive(1, 3)
    arrive_y(2, 2)
    local[5].wait()
    arrive_c(1, 0)
    arrive_c(2, 0)
    project(s)
    arrive(2, 3)
    arrive_y(1, 3)
    arrive_c(1, 1)
    arrive_c(2, 1)
    each(1, project)
    arrive_c(1, 2)
    arrive_c(2, 2)
    arrive_y(2, 3)
    each(2, project)
    arrive_c(1, 3)
    arrive_c(2, 3)
    each(3, project)

    ends_row = jnp.dot(
        jnp.broadcast_to(lens_row.astype(f32), (8, count)).astype(bf16),
        jnp.where(iota((count, count), 0) <= iota((count, count), 1), 1.0, 0.0).astype(bf16),
        preferred_element_type=f32,
    )[0:1]
    sq_copy.wait_recv()
    square = jnp.sum(sq[...] + sq_in[...], axis=1, keepdims=True)
    scale = lax.rsqrt(square / D + 1e-06)

    def finish(slot, carry):
        part_copy(slot).wait_recv()
        kv[slot] = ((part[slot] + part_in[slot].astype(f32)) * scale).astype(bf16)
        return carry

    lax.fori_loop(0, n, finish, 0)
    local[3].wait()
    xc_copy(1).wait_recv()
    keys_n = count + HALO
    key = iota((1, keys_n), 1)
    key = jnp.where(key < count, key, key - keys_n).astype(f32)
    first = me == 0
    low_half = iota((keys_n, 128), 1) < HEAD_DIM

    def y_copy(r):
        at = pl.ds(pl.multiple_of(t * half + r * ROWS, ROWS), ROWS)
        return remote(y_out.at[pl.ds(r * ROWS, ROWS)], out_ref.at[at], y_send.at[r], y_recv.at[r], x_peer)

    for r in range(half // ROWS):
        place = (iota((ROWS, 1), 0) + (t * half + r * ROWS)).astype(f32)
        patch = jnp.sum(jnp.where(ends_row <= place, 1.0, 0.0), axis=1, keepdims=True)
        floor = jnp.where(first, jnp.maximum(patch - WIN, -1.0), patch - WIN)
        bias = jnp.where((key <= patch) & (key > floor), 0.0, -1e30)

        def heads(slot, carry):
            at = pl.ds(pl.multiple_of(slot * 128, 128), 128)
            q = query[pl.ds(r * ROWS, ROWS), at]
            keys, values = kv[slot, :, pl.ds(0, 128)], kv[slot, :, pl.ds(128, 128)]
            result = jnp.zeros((ROWS, 128), f32)
            for low in (True, False):
                pick_head = low_half if low else jnp.logical_not(low_half)
                kh = jnp.where(pick_head, keys, jnp.zeros_like(keys))
                vh = jnp.where(pick_head, values, jnp.zeros_like(values))
                scores = lax.dot_general(q, kh, (((1,), (1,)), ((), ())), preferred_element_type=f32)
                scores = scores * (1.0 / math.sqrt(HEAD_DIM)) + bias
                expo = jnp.exp(scores - jnp.max(scores, axis=1, keepdims=True))
                weights = (expo / jnp.sum(expo, axis=1, keepdims=True)).astype(bf16)
                result = result + jnp.dot(weights, vh, preferred_element_type=f32)
            att[pl.ds(r * ROWS, ROWS), at] = result.astype(bf16)
            return carry

        lax.fori_loop(0, n, heads, 0)
        at = pl.ds(pl.multiple_of(t * half + r * ROWS, ROWS), ROWS)
        a = att[pl.ds(r * ROWS, ROWS), :]
        for who in (1 - t, t):
            at_cols = pl.ds(pl.multiple_of(who * cols, cols), cols)
            value = br[at, at_cols].astype(f32) + jnp.dot(a, wo[who], preferred_element_type=f32)
            if who is t:
                out_ref[at, :] = value.astype(bf16)
            else:
                y_out[pl.ds(r * ROWS, ROWS), :] = value.astype(bf16)
                y_copy(r).start()

    for r in range(half // ROWS):
        y_copy(r).wait()
    for kind in range(3):
        pl.when(s + 1 < n_seq)(lambda: right(kind, s, True).wait_send())
        pl.when(s > 0)(lambda: left(kind, s, True).wait_send())
        for h in range(2):
            core(kind, s, h, True).wait_send()
        for k in range(1, n_seq):
            def sent(z, from_left):
                if from_left:
                    pl.when(s + 1 < n_seq)(lambda: right(kind, z).wait_send())
                else:
                    pl.when(s > 0)(lambda: left(kind, z).wait_send())
                across(kind, z).wait_send()
                core(kind, z, 0).wait_send()
                core(kind, z, 1).wait_send()
            each(k, sent)
    for i in range(1, n):
        stream_copy(i).wait_send()
    for i in range(2):
        x_copy(i).wait_send()
        xc_copy(i).wait_send()
    halo_pooled.wait_send()
    halo_stream.wait_send()
    sq_copy.wait_send()
    lax.fori_loop(0, n, lambda slot, carry: (part_copy(slot).wait_send(), carry)[1], 0)


def fused(
    byte_rows, patch_lengths, patch_owner, patch_stream, w_in, norm_gain, w_kv, w_query, w_out
):
    n_seq = lax.axis_size("seq")
    n = n_seq * 2
    byte_count, dl = byte_rows.shape
    count = patch_owner.shape[0]
    depth, width = w_in.shape
    cols = w_query.shape[1]
    half = byte_count // 2
    tall = count + HALO
    chunks = half // ROWS
    any_spec, vmem = pl.BlockSpec(memory_space=pl.ANY), pl.BlockSpec(memory_space=pltpu.VMEM)
    dma = pltpu.SemaphoreType.DMA
    return pl.pallas_call(
        functools.partial(fused_kernel, n_seq),
        out_shape=jax.ShapeDtypeStruct((byte_count, cols), bf16),
        in_specs=[any_spec, vmem, vmem, vmem, any_spec, any_spec, vmem, any_spec, any_spec, any_spec],
        out_specs=vmem,
        scratch_shapes=[
            pltpu.VMEM((n * depth, width), bf16),
            pltpu.VMEM((n, 2, width, 128), bf16),
            pltpu.VMEM(patch_stream.shape, bf16),
            pltpu.VMEM((byte_count, dl), bf16),
            pltpu.VMEM((2, dl, cols), bf16),
            pltpu.VMEM((2, dl, cols), bf16),
            pltpu.VMEM((tall, dl), bf16),
            pltpu.VMEM((tall, width), f32),
            pltpu.VMEM((tall, width), bf16),
            pltpu.VMEM((HALO, width), bf16),
            pltpu.VMEM((HALO, width), bf16),
            pltpu.VMEM((n, tall, 256), f32),
            pltpu.VMEM((n, tall, 256), bf16),
            pltpu.VMEM((n, tall, 256), bf16),
            pltpu.VMEM((n, tall, 256), bf16),
            pltpu.VMEM((tall, 128), f32),
            pltpu.VMEM((tall, 128), f32),
            pltpu.VMEM((half, dl), bf16),
            pltpu.VMEM((half, dl), bf16),
            pltpu.VMEM((half, cols), bf16),
            dma((3, n, 2)),
            dma((3, n_seq)),
            dma((3, n_seq)),
            dma((3, n_seq)),
            dma((3, n_seq, 2)),
            dma((6,)),
            dma((n,)),
            dma((n,)),
            dma((2,)),
            dma((2,)),
            dma((2,)),
            dma((2,)),
            dma((2,)),
            dma((2,)),
            dma((n + 1,)),
            dma((n + 1,)),
            dma((chunks,)),
            dma((chunks,)),
        ],
        compiler_params=pltpu.CompilerParams(
            collective_id=0, has_side_effects=True, vmem_limit_bytes=56 * 1024 * 1024
        ),
        cost_estimate=pl.CostEstimate(flops=9 * 10**9, bytes_accessed=8 * 10**6, transcendentals=2 * 10**6),
    )(
        byte_rows, patch_lengths, patch_owner, patch_owner.reshape(1, count), patch_stream, w_in,
        norm_gain.reshape(1, width), w_kv, w_query, w_out,
    )


def solution(mesh):
    sizes = mesh.shape
    fits = sizes["groups"] == 2 and sizes["tp"] == 2 and sizes["dp"] == 2 and sizes["seq"] == 4
    return jax.shard_map(
        fused if fits else local,
        mesh=mesh,
        in_specs=(
            P(("groups", "seq", "dp"), None),
            P(("groups", "seq", "dp"), None),
            P(("groups", "seq", "dp"), None),
            P(("groups", "seq", "dp"), "tp"),
            P(("seq", "dp"), "tp"),
            P("tp"),
            P(None, "tp", ("seq", "dp")),
            P(None, "tp"),
            P(None, "tp"),
        ),
        out_specs=P(("groups", "seq", "dp"), "tp"),
        check_vma=False,
    )
```

```python
import functools
import math

import jax
import jax.numpy as jnp
from jax import lax
from jax.experimental import pallas as pl
from jax.experimental.pallas import tpu as pltpu
from jax.sharding import PartitionSpec as P

D = 4096
HEAD_DIM = 64
WIN = 8


def shifted(block, axis, distance):
    devices = range(lax.axis_size(axis))
    route = [(i - distance, i) for i in devices if i - distance in devices]
    return lax.ppermute(block, axis, route)


def local(
    byte_rows, patch_lengths, patch_owner, patch_stream, w_in, norm_gain, w_kv, w_query, w_out
):
    sources = lax.axis_size(("seq", "dp"))
    lens = patch_lengths[0]
    count = lens.shape[0]
    byte_count = byte_rows.shape[0]
    slots = patch_stream.shape[0]
    cap = slots // sources
    quarter = w_query.shape[1]
    ends = jnp.cumsum(lens)
    starts = ends - lens
    places = jnp.arange(byte_count, dtype=jnp.int32)
    members = ((places[None, :] >= starts[:, None]) & (places[None, :] < ends[:, None])).astype(
        jnp.bfloat16
    )
    sums = jnp.dot(members, byte_rows, preferred_element_type=jnp.float32)
    pooled = (sums / lens[:, None].astype(jnp.float32)).astype(jnp.bfloat16)
    owners = patch_owner[:, 0]
    match = (owners[:, None] == jnp.arange(sources, dtype=jnp.int32)[None, :]).astype(jnp.int32)
    ranking = jnp.sum(jnp.cumsum(match, axis=0) * match, axis=1) - 1
    targets = owners * cap + ranking
    dispatch = (jnp.arange(slots, dtype=jnp.int32)[:, None] == targets[None, :]).astype(
        jnp.bfloat16
    )
    outgoing = jnp.dot(dispatch, pooled, preferred_element_type=jnp.float32).astype(jnp.bfloat16)
    outgoing = outgoing.reshape(sources, cap, outgoing.shape[1])
    arrived = lax.all_to_all(outgoing, ("seq", "dp"), split_axis=0, concat_axis=0, tiled=True)
    inputs = arrived.reshape(slots, arrived.shape[2])
    mixed = jnp.dot(
        inputs,
        lax.all_gather(w_in, ("seq", "dp"), axis=0, tiled=True),
        preferred_element_type=jnp.float32,
    )
    mixed = mixed + patch_stream.astype(jnp.float32)
    squares = lax.psum(jnp.sum(mixed * mixed, axis=1), "tp")
    normed = (mixed * lax.rsqrt(squares / D + 1e-06)[:, None] * norm_gain[None, :]).astype(
        jnp.bfloat16
    )
    partial_kv = jnp.einsum(
        "sd,kdc->skc",
        normed,
        lax.all_gather(w_kv, ("seq", "dp"), axis=2, tiled=True),
        preferred_element_type=jnp.float32,
    )
    kv_slots = lax.psum_scatter(partial_kv, "tp", scatter_dimension=2, tiled=True).astype(
        jnp.bfloat16
    )
    returned = lax.all_to_all(
        kv_slots.reshape(sources, cap, 2, quarter),
        ("seq", "dp"),
        split_axis=0,
        concat_axis=0,
        tiled=True,
    )
    kv_patch = jnp.einsum(
        "sp,skc->pkc",
        dispatch,
        returned.reshape(slots, 2, quarter),
        preferred_element_type=jnp.float32,
    ).astype(jnp.bfloat16)
    prior = shifted(kv_patch[count - (WIN - 1) :], ("seq", "dp"), 1)
    window_kv = jnp.concatenate([prior, kv_patch], axis=0)
    query = jnp.dot(byte_rows, w_query, preferred_element_type=jnp.float32).astype(jnp.bfloat16)
    heads = quarter // HEAD_DIM
    mine = jnp.sum((ends[None, :] <= places[:, None]).astype(jnp.int32), axis=1)
    key_index = jnp.arange(count + WIN - 1, dtype=jnp.int32) - (WIN - 1)
    first_block = lax.axis_index(("seq", "dp")) == 0
    allowed = (key_index[None, :] <= mine[:, None]) & (key_index[None, :] > mine[:, None] - WIN)
    allowed = allowed & ((key_index[None, :] >= 0) | jnp.logical_not(first_block))
    queries = query.reshape(byte_count, heads, HEAD_DIM)
    keys = window_kv[:, 0].reshape(-1, heads, HEAD_DIM)
    values = window_kv[:, 1].reshape(-1, heads, HEAD_DIM)
    scores = jnp.einsum("ihe,khe->hik", queries, keys, preferred_element_type=jnp.float32) * (
        1.0 / math.sqrt(HEAD_DIM)
    )
    scores = jnp.where(allowed[None, :, :], scores, -1e30)
    top = jnp.max(scores, axis=-1, keepdims=True)
    expo = jnp.exp(scores - top)
    weights = (expo / jnp.sum(expo, axis=-1, keepdims=True)).astype(jnp.bfloat16)
    attended = jnp.einsum("hik,khe->ihe", weights, values, preferred_element_type=jnp.float32)
    attended = attended.astype(jnp.bfloat16).reshape(byte_count, quarter)
    projected = jnp.dot(
        lax.all_gather(attended, "tp", axis=1, tiled=True),
        w_out,
        preferred_element_type=jnp.float32,
    )
    residual = lax.dynamic_slice_in_dim(byte_rows, lax.axis_index("tp") * quarter, quarter, 1)
    return (residual.astype(jnp.float32) + projected).astype(jnp.bfloat16)


MESH = pl.DeviceIdType.MESH
HALO = 16
ROWS = 256
bf16, f32 = jnp.bfloat16, jnp.float32


def iota(shape, axis):
    return lax.broadcasted_iota(jnp.int32, shape, axis)


def fused_kernel(
    n_seq,
    rows_ref, lens_ref, own_col_ref, own_row_ref, stream_ref, w_in_ref, gain_ref, w_kv_ref,
    w_query_ref, w_out_ref, out_ref,
    win, wkv, arr, br, wq, wo, pooled, mixed, nrm, hs_out, hs_in, part, part_out, part_in,
    kv, sq, sq_in, query, att, bias,
    recv, send_r, send_l, send_y, send_c, local_sem, st_send, st_recv, x_send, x_recv,
    xc_send, xc_recv, h_send, h_recv, p_send, p_recv,
):
    g, s = lax.axis_index("groups"), lax.axis_index("seq")
    t, d = lax.axis_index("tp"), lax.axis_index("dp")
    n = n_seq * 2
    me = s * 2 + d
    count = own_col_ref.shape[0]
    byte_count, dl = rows_ref.shape
    depth, width = w_in_ref.shape
    cap = stream_ref.shape[0] // n
    cols = w_query_ref.shape[1]
    hd = depth // 2
    hw = width // 2
    y_peer, c_peer, x_peer = {"groups": 1 - g}, {"dp": 1 - d}, {"tp": 1 - t}

    barrier = pltpu.get_barrier_semaphore()

    def other(i):
        b = lax.rem(me + i, n)
        return b, {"seq": b // 2, "dp": lax.rem(b, 2)}

    for i in range(1, n):
        pl.semaphore_signal(barrier, inc=1, device_id=other(i)[1], device_id_type=MESH)
    pl.semaphore_signal(barrier, inc=1, device_id=y_peer, device_id_type=MESH)
    pl.semaphore_signal(barrier, inc=1, device_id=x_peer, device_id_type=MESH)

    local = []

    def bring(src, dst):
        copy = pltpu.make_async_copy(src, dst, local_sem.at[len(local)])
        copy.start()
        local.append(copy)

    bring(rows_ref, br)
    bring(stream_ref.at[pl.ds(pl.multiple_of(me * cap, cap), cap)], arr.at[pl.ds(pl.multiple_of(me * cap, cap), cap)])
    bring(w_query_ref, wq.at[t])
    bring(w_out_ref, wo)
    bring(w_in_ref, win.at[pl.ds(pl.multiple_of(me * depth, depth), depth)])
    bring(w_kv_ref, wkv.at[me])
    pl.semaphore_wait(barrier, n + 1)

    def remote(src, dst, send, arrive, where):
        return pltpu.make_async_remote_copy(
            src_ref=src, dst_ref=dst, send_sem=send, recv_sem=arrive, device_id=where, device_id_type=MESH
        )

    def held(kind, slot, h):
        if kind == 0:
            return win.at[pl.ds(pl.multiple_of(slot * depth + h * hd, hd), hd)]
        return wkv.at[slot, h, pl.ds((kind - 1) * hw, hw)]

    def own(kind, h):
        if kind == 0:
            return w_in_ref.at[pl.ds(pl.multiple_of(h * hd, hd), hd)]
        return w_kv_ref.at[h, pl.ds((kind - 1) * hw, hw)]

    def piece(kind, z, h, send, where, mine=False, core=None):
        slot = z * 2 + (d if core is None else core)
        dst = held(kind, slot, h)
        return remote(own(kind, h) if mine else dst, dst, send, recv.at[kind, slot, h], where)

    def right(kind, z, mine=False):
        return piece(kind, z, g, send_r.at[kind, z], {"seq": jnp.minimum(s + 1, n_seq - 1)}, mine)

    def left(kind, z, mine=False):
        return piece(kind, z, g, send_l.at[kind, z], {"seq": jnp.maximum(s - 1, 0)}, mine)

    def across(kind, z):
        return piece(kind, z, g, send_y.at[kind, z], y_peer)

    def core(kind, z, h, mine=False):
        return piece(kind, z, h, send_c.at[kind, z, h], c_peer, mine)

    def ends_of_line(kind):
        pl.when(s + 1 < n_seq)(lambda: right(kind, s, True).start())
        pl.when(s > 0)(lambda: left(kind, s, True).start())

    def each(k, fn):
        pl.when(s - k >= 0)(lambda: fn(s - k, True))
        pl.when(s + k < n_seq)(lambda: fn(s + k, False))

    def arrive(kind, k):
        def one(z, from_left):
            piece(kind, z, g, send_y.at[kind, z], y_peer).wait_recv()
            if from_left:
                pl.when(s + 1 < n_seq)(lambda: right(kind, z).start())
            else:
                pl.when(s > 0)(lambda: left(kind, z).start())
            across(kind, z).start()
            core(kind, z, g).start()
        each(k, one)

    def arrive_y(kind, k):
        def one(z, _):
            piece(kind, z, 1 - g, send_y.at[kind, z], y_peer).wait_recv()
            core(kind, z, 1 - g).start()
        each(k, one)

    def arrive_c(kind, k):
        def one(z, _=None):
            for h in range(2):
                piece(kind, z, h, send_c.at[kind, z, h], c_peer, core=1 - d).wait_recv()
        one(s) if k == 0 else each(k, one)

    ends_of_line(0)

    def stream_copy(i):
        b, where = other(i)
        src = stream_ref.at[pl.ds(pl.multiple_of(b * cap, cap), cap)]
        dst = arr.at[pl.ds(pl.multiple_of(me * cap, cap), cap)]
        return remote(src, dst, st_send.at[i], st_recv.at[i], where)

    for i in range(1, n):
        stream_copy(i).start()
    dh = dl // 2
    mine_rows = pl.ds(pl.multiple_of(d * dh, dh), dh)

    def x_copy(i):
        return remote(w_query_ref.at[mine_rows], wq.at[t, mine_rows], x_send.at[i], x_recv.at[i], x_peer)

    def xc_copy(i):
        dst = wq.at[1 - t, mine_rows]
        return remote(dst, dst, xc_send.at[i], xc_recv.at[i], c_peer)

    x_copy(0).start()
    for kind in range(3):
        for h in range(2):
            core(kind, s, h, True).start()
    ends_of_line(1)
    ends_of_line(2)

    local[0].wait()
    lens_row = lens_ref[...]
    tri = iota((count, count), 1) <= iota((count, count), 0)
    ends_col = jnp.sum(jnp.where(tri, lens_row, 0).astype(f32), axis=1, keepdims=True)
    lens_col = jnp.sum(
        jnp.where(iota((count, count), 0) == iota((count, count), 1), lens_row, 0).astype(f32), axis=1, keepdims=True
    )
    places = iota((count, byte_count), 1).astype(f32)
    members = jnp.where((places >= ends_col - lens_col) & (places < ends_col), 1.0, 0.0).astype(bf16)
    sums = jnp.dot(members, br[...], preferred_element_type=f32)
    pooled[pl.ds(0, count)] = (sums / lens_col).astype(bf16)
    _, following = other(1)
    halo_pooled = remote(
        pooled.at[pl.ds(count - HALO, HALO)], pooled.at[pl.ds(count, HALO)], h_send.at[0], h_recv.at[0], following
    )
    halo_pooled.start()

    arrive(0, 1)
    arrive(1, 1)
    x_copy(0).wait_recv()
    xc_copy(0).start()
    arrive(2, 1)
    arrive_y(0, 1)
    arrive(0, 2)
    local[2].wait()
    xc_copy(0).wait_recv()
    for part_t in range(2):
        query[:, part_t * cols:(part_t + 1) * cols] = jnp.dot(
            br[...], wq[part_t], preferred_element_type=f32
        ).astype(bf16)
    arrive_y(1, 1)
    arrive(1, 2)
    arrive_y(2, 1)
    arrive(2, 2)
    arrive_y(0, 2)
    arrive(0, 3)

    for i in range(1, n):
        stream_copy(i).wait_recv()
    local[1].wait()
    owner = own_col_ref[...]
    same = (owner == own_row_ref[...]) & (iota((count, count), 1) < iota((count, count), 0))
    ranking = jnp.sum(jnp.where(same, 1.0, 0.0), axis=1, keepdims=True)
    target = owner.astype(f32) * cap + ranking
    pick = jnp.where(iota((count, n * cap), 1).astype(f32) == target, 1.0, 0.0).astype(bf16)
    mixed[pl.ds(0, count)] = jnp.dot(pick, arr[...], preferred_element_type=f32)
    hs_out[...] = mixed[pl.ds(count - HALO, HALO)].astype(bf16)
    halo_stream = remote(hs_out, hs_in, h_send.at[1], h_recv.at[1], following)
    halo_stream.start()
    arrive_y(1, 2)
    arrive_y(0, 3)
    for k in range(n_seq):
        arrive_c(0, k)
    local[4].wait()
    halo_pooled.wait_recv()
    halo_stream.wait_recv()
    mixed[pl.ds(count, HALO)] = hs_in[...].astype(f32)
    step = 512
    total = jnp.zeros((count + HALO, 128), f32)
    for c in range(width // step):
        at = pl.ds(c * step, step)
        now = mixed[:, at] + jnp.dot(pooled[...], win[:, at], preferred_element_type=f32)
        nrm[:, at] = (now * gain_ref[:, at]).astype(bf16)
        for j in range(step // 128):
            lane = now[:, j * 128:(j + 1) * 128]
            total = total + lane * lane
    sq[...] = total
    sq_copy = remote(sq, sq_in, p_send.at[n], p_recv.at[n], x_peer)
    sq_copy.start()

    def part_copy(slot):
        return remote(part_out.at[slot], part_in.at[slot], p_send.at[slot], p_recv.at[slot], x_peer)

    def project(z, _=None):
        for c in range(2):
            slot = z * 2 + c
            for h in range(2):
                val = jnp.dot(nrm[...], wkv[slot, h], preferred_element_type=f32)
                part[slot, :, pl.ds(h * 128, 128)] = val
                part_out[slot, :, pl.ds(h * 128, 128)] = val.astype(bf16)
            part_copy(slot).start()

    ends_row = jnp.dot(
        jnp.broadcast_to(lens_row.astype(f32), (8, count)).astype(bf16),
        jnp.where(iota((count, count), 0) <= iota((count, count), 1), 1.0, 0.0).astype(bf16),
        preferred_element_type=f32,
    )[0:1]
    keys_n = count + HALO
    key = iota((1, keys_n), 1)
    key = jnp.where(key < count, key, key - keys_n).astype(f32)
    for r in range(byte_count // ROWS):
        place = (iota((ROWS, 1), 0) + r * ROWS).astype(f32)
        patch = jnp.sum(jnp.where(ends_row <= place, 1.0, 0.0), axis=1, keepdims=True)
        floor = jnp.where(me == 0, jnp.maximum(patch - WIN, -1.0), patch - WIN)
        bias[pl.ds(r * ROWS, ROWS)] = jnp.where((key <= patch) & (key > floor), 0.0, -1e30)

    def attend(z, _=None):
        square = jnp.sum(sq[...] + sq_in[...], axis=1, keepdims=True)
        scale = lax.rsqrt(square / D + 1e-06)
        low_half = iota((keys_n, 128), 1) < HEAD_DIM
        for c in range(2):
            slot = z * 2 + c
            part_copy(slot).wait_recv()
            kv[slot] = ((part[slot] + part_in[slot].astype(f32)) * scale).astype(bf16)
            at = pl.ds(pl.multiple_of(slot * 128, 128), 128)
            keys, values = kv[slot, :, pl.ds(0, 128)], kv[slot, :, pl.ds(128, 128)]

            def chunk(r, carry):
                rows = pl.ds(pl.multiple_of(r * ROWS, ROWS), ROWS)
                q, shut = query[rows, at], bias[rows, :]
                result = jnp.zeros((ROWS, 128), f32)
                for low in (True, False):
                    pick_head = low_half if low else jnp.logical_not(low_half)
                    kh = jnp.where(pick_head, keys, jnp.zeros_like(keys))
                    vh = jnp.where(pick_head, values, jnp.zeros_like(values))
                    scores = lax.dot_general(q, kh, (((1,), (1,)), ((), ())), preferred_element_type=f32)
                    scores = scores * (1.0 / math.sqrt(HEAD_DIM)) + shut
                    expo = jnp.exp(scores - jnp.max(scores, axis=1, keepdims=True))
                    weights = (expo / jnp.sum(expo, axis=1, keepdims=True)).astype(bf16)
                    result = result + jnp.dot(weights, vh, preferred_element_type=f32)
                att[rows, at] = result.astype(bf16)
                return carry

            lax.fori_loop(0, byte_count // ROWS, chunk, 0)

    arrive(1, 3)
    arrive_y(2, 2)
    local[5].wait()
    arrive_c(1, 0)
    arrive_c(2, 0)
    project(s)
    arrive(2, 3)
    arrive_y(1, 3)
    arrive_c(1, 1)
    arrive_c(2, 1)
    each(1, project)
    sq_copy.wait_recv()
    arrive_c(1, 2)
    arrive_c(2, 2)
    arrive_y(2, 3)
    each(2, project)
    attend(s)
    each(1, attend)
    arrive_c(1, 3)
    arrive_c(2, 3)
    each(3, project)
    each(2, attend)
    each(3, attend)
    local[3].wait()
    my_cols = pl.ds(pl.multiple_of(t * cols, cols), cols)
    for r in range(byte_count // ROWS):
        rows = pl.ds(r * ROWS, ROWS)
        value = br[rows, my_cols].astype(f32) + jnp.dot(att[rows, :], wo[...], preferred_element_type=f32)
        out_ref[rows, :] = value.astype(bf16)

    for kind in range(3):
        pl.when(s + 1 < n_seq)(lambda: right(kind, s, True).wait_send())
        pl.when(s > 0)(lambda: left(kind, s, True).wait_send())
        for h in range(2):
            core(kind, s, h, True).wait_send()
        for k in range(1, n_seq):
            def sent(z, from_left):
                if from_left:
                    pl.when(s + 1 < n_seq)(lambda: right(kind, z).wait_send())
                else:
                    pl.when(s > 0)(lambda: left(kind, z).wait_send())
                across(kind, z).wait_send()
                core(kind, z, 0).wait_send()
                core(kind, z, 1).wait_send()
            each(k, sent)
    for i in range(1, n):
        stream_copy(i).wait_send()
    x_copy(0).wait_send()
    xc_copy(0).wait_send()
    halo_pooled.wait_send()
    halo_stream.wait_send()
    sq_copy.wait_send()
    lax.fori_loop(0, n, lambda slot, carry: (part_copy(slot).wait_send(), carry)[1], 0)


def fused(
    byte_rows, patch_lengths, patch_owner, patch_stream, w_in, norm_gain, w_kv, w_query, w_out
):
    n_seq = lax.axis_size("seq")
    n = n_seq * 2
    byte_count, dl = byte_rows.shape
    count = patch_owner.shape[0]
    depth, width = w_in.shape
    cols = w_query.shape[1]
    tall = count + HALO
    any_spec, vmem = pl.BlockSpec(memory_space=pl.ANY), pl.BlockSpec(memory_space=pltpu.VMEM)
    dma = pltpu.SemaphoreType.DMA
    return pl.pallas_call(
        functools.partial(fused_kernel, n_seq),
        out_shape=jax.ShapeDtypeStruct((byte_count, cols), bf16),
        in_specs=[any_spec, vmem, vmem, vmem, any_spec, any_spec, vmem, any_spec, any_spec, any_spec],
        out_specs=vmem,
        scratch_shapes=[
            pltpu.VMEM((n * depth, width), bf16),
            pltpu.VMEM((n, 2, width, 128), bf16),
            pltpu.VMEM(patch_stream.shape, bf16),
            pltpu.VMEM((byte_count, dl), bf16),
            pltpu.VMEM((2, dl, cols), bf16),
            pltpu.VMEM((dl, cols), bf16),
            pltpu.VMEM((tall, dl), bf16),
            pltpu.VMEM((tall, width), f32),
            pltpu.VMEM((tall, width), bf16),
            pltpu.VMEM((HALO, width), bf16),
            pltpu.VMEM((HALO, width), bf16),
            pltpu.VMEM((n, tall, 256), f32),
            pltpu.VMEM((n, tall, 256), bf16),
            pltpu.VMEM((n, tall, 256), bf16),
            pltpu.VMEM((n, tall, 256), bf16),
            pltpu.VMEM((tall, 128), f32),
            pltpu.VMEM((tall, 128), f32),
            pltpu.VMEM((byte_count, dl), bf16),
            pltpu.VMEM((byte_count, dl), bf16),
            pltpu.VMEM((byte_count, tall), f32),
            dma((3, n, 2)),
            dma((3, n_seq)),
            dma((3, n_seq)),
            dma((3, n_seq)),
            dma((3, n_seq, 2)),
            dma((6,)),
            dma((n,)),
            dma((n,)),
            dma((2,)),
            dma((2,)),
            dma((2,)),
            dma((2,)),
            dma((2,)),
            dma((2,)),
            dma((n + 1,)),
            dma((n + 1,)),
        ],
        compiler_params=pltpu.CompilerParams(
            collective_id=0, has_side_effects=True, vmem_limit_bytes=56 * 1024 * 1024
        ),
        cost_estimate=pl.CostEstimate(flops=9 * 10**9, bytes_accessed=8 * 10**6, transcendentals=2 * 10**6),
    )(
        byte_rows, patch_lengths, patch_owner, patch_owner.reshape(1, count), patch_stream, w_in,
        norm_gain.reshape(1, width), w_kv, w_query, w_out,
    )


def solution(mesh):
    sizes = mesh.shape
    fits = sizes["groups"] == 2 and sizes["tp"] == 2 and sizes["dp"] == 2 and sizes["seq"] == 4
    return jax.shard_map(
        fused if fits else local,
        mesh=mesh,
        in_specs=(
            P(("groups", "seq", "dp"), None),
            P(("groups", "seq", "dp"), None),
            P(("groups", "seq", "dp"), None),
            P(("groups", "seq", "dp"), "tp"),
            P(("seq", "dp"), "tp"),
            P("tp"),
            P(None, "tp", ("seq", "dp")),
            P(None, "tp"),
            P(None, "tp"),
        ),
        out_specs=P(("groups", "seq", "dp"), "tp"),
        check_vma=False,
    )
```

```python
import functools
import math

import jax
import jax.numpy as jnp
from jax import lax
from jax.experimental import pallas as pl
from jax.experimental.pallas import tpu as pltpu
from jax.sharding import PartitionSpec as P

D = 4096
HEAD_DIM = 64
WIN = 8


def shifted(block, axis, distance):
    devices = range(lax.axis_size(axis))
    route = [(i - distance, i) for i in devices if i - distance in devices]
    return lax.ppermute(block, axis, route)


def local(
    byte_rows, patch_lengths, patch_owner, patch_stream, w_in, norm_gain, w_kv, w_query, w_out
):
    sources = lax.axis_size(("seq", "dp"))
    lens = patch_lengths[0]
    count = lens.shape[0]
    byte_count = byte_rows.shape[0]
    slots = patch_stream.shape[0]
    cap = slots // sources
    quarter = w_query.shape[1]
    ends = jnp.cumsum(lens)
    starts = ends - lens
    places = jnp.arange(byte_count, dtype=jnp.int32)
    members = ((places[None, :] >= starts[:, None]) & (places[None, :] < ends[:, None])).astype(
        jnp.bfloat16
    )
    sums = jnp.dot(members, byte_rows, preferred_element_type=jnp.float32)
    pooled = (sums / lens[:, None].astype(jnp.float32)).astype(jnp.bfloat16)
    owners = patch_owner[:, 0]
    match = (owners[:, None] == jnp.arange(sources, dtype=jnp.int32)[None, :]).astype(jnp.int32)
    ranking = jnp.sum(jnp.cumsum(match, axis=0) * match, axis=1) - 1
    targets = owners * cap + ranking
    dispatch = (jnp.arange(slots, dtype=jnp.int32)[:, None] == targets[None, :]).astype(
        jnp.bfloat16
    )
    outgoing = jnp.dot(dispatch, pooled, preferred_element_type=jnp.float32).astype(jnp.bfloat16)
    outgoing = outgoing.reshape(sources, cap, outgoing.shape[1])
    arrived = lax.all_to_all(outgoing, ("seq", "dp"), split_axis=0, concat_axis=0, tiled=True)
    inputs = arrived.reshape(slots, arrived.shape[2])
    mixed = jnp.dot(
        inputs,
        lax.all_gather(w_in, ("seq", "dp"), axis=0, tiled=True),
        preferred_element_type=jnp.float32,
    )
    mixed = mixed + patch_stream.astype(jnp.float32)
    squares = lax.psum(jnp.sum(mixed * mixed, axis=1), "tp")
    normed = (mixed * lax.rsqrt(squares / D + 1e-06)[:, None] * norm_gain[None, :]).astype(
        jnp.bfloat16
    )
    partial_kv = jnp.einsum(
        "sd,kdc->skc",
        normed,
        lax.all_gather(w_kv, ("seq", "dp"), axis=2, tiled=True),
        preferred_element_type=jnp.float32,
    )
    kv_slots = lax.psum_scatter(partial_kv, "tp", scatter_dimension=2, tiled=True).astype(
        jnp.bfloat16
    )
    returned = lax.all_to_all(
        kv_slots.reshape(sources, cap, 2, quarter),
        ("seq", "dp"),
        split_axis=0,
        concat_axis=0,
        tiled=True,
    )
    kv_patch = jnp.einsum(
        "sp,skc->pkc",
        dispatch,
        returned.reshape(slots, 2, quarter),
        preferred_element_type=jnp.float32,
    ).astype(jnp.bfloat16)
    prior = shifted(kv_patch[count - (WIN - 1) :], ("seq", "dp"), 1)
    window_kv = jnp.concatenate([prior, kv_patch], axis=0)
    query = jnp.dot(byte_rows, w_query, preferred_element_type=jnp.float32).astype(jnp.bfloat16)
    heads = quarter // HEAD_DIM
    mine = jnp.sum((ends[None, :] <= places[:, None]).astype(jnp.int32), axis=1)
    key_index = jnp.arange(count + WIN - 1, dtype=jnp.int32) - (WIN - 1)
    first_block = lax.axis_index(("seq", "dp")) == 0
    allowed = (key_index[None, :] <= mine[:, None]) & (key_index[None, :] > mine[:, None] - WIN)
    allowed = allowed & ((key_index[None, :] >= 0) | jnp.logical_not(first_block))
    queries = query.reshape(byte_count, heads, HEAD_DIM)
    keys = window_kv[:, 0].reshape(-1, heads, HEAD_DIM)
    values = window_kv[:, 1].reshape(-1, heads, HEAD_DIM)
    scores = jnp.einsum("ihe,khe->hik", queries, keys, preferred_element_type=jnp.float32) * (
        1.0 / math.sqrt(HEAD_DIM)
    )
    scores = jnp.where(allowed[None, :, :], scores, -1e30)
    top = jnp.max(scores, axis=-1, keepdims=True)
    expo = jnp.exp(scores - top)
    weights = (expo / jnp.sum(expo, axis=-1, keepdims=True)).astype(jnp.bfloat16)
    attended = jnp.einsum("hik,khe->ihe", weights, values, preferred_element_type=jnp.float32)
    attended = attended.astype(jnp.bfloat16).reshape(byte_count, quarter)
    projected = jnp.dot(
        lax.all_gather(attended, "tp", axis=1, tiled=True),
        w_out,
        preferred_element_type=jnp.float32,
    )
    residual = lax.dynamic_slice_in_dim(byte_rows, lax.axis_index("tp") * quarter, quarter, 1)
    return (residual.astype(jnp.float32) + projected).astype(jnp.bfloat16)


MESH = pl.DeviceIdType.MESH
HALO = 16
ROWS = 256
bf16, f32 = jnp.bfloat16, jnp.float32


def iota(shape, axis):
    return lax.broadcasted_iota(jnp.int32, shape, axis)


def fused_kernel(
    n_seq,
    rows_ref, lens_ref, own_col_ref, own_row_ref, stream_ref, w_in_ref, gain_ref, w_kv_ref,
    w_query_ref, w_out_ref, out_ref,
    win, wkv, arr, br, wq, wo, pooled, mixed, nrm, hs_out, hs_in, part, part_out, part_in,
    kv, sq, sq_in, query, att, bias,
    recv, send_r, send_l, send_y, send_c, local_sem, st_send, st_recv, x_send, x_recv,
    xc_send, xc_recv, h_send, h_recv, p_send, p_recv,
):
    g, s = lax.axis_index("groups"), lax.axis_index("seq")
    t, d = lax.axis_index("tp"), lax.axis_index("dp")
    n = n_seq * 2
    me = s * 2 + d
    count = own_col_ref.shape[0]
    byte_count, dl = rows_ref.shape
    depth, width = w_in_ref.shape
    cap = stream_ref.shape[0] // n
    cols = w_query_ref.shape[1]
    hd = depth // 2
    hw = width // 2
    y_peer, c_peer, x_peer = {"groups": 1 - g}, {"dp": 1 - d}, {"tp": 1 - t}

    barrier = pltpu.get_barrier_semaphore()

    def other(i):
        b = lax.rem(me + i, n)
        return b, {"seq": b // 2, "dp": lax.rem(b, 2)}

    for i in range(1, n):
        pl.semaphore_signal(barrier, inc=1, device_id=other(i)[1], device_id_type=MESH)
    pl.semaphore_signal(barrier, inc=1, device_id=y_peer, device_id_type=MESH)
    pl.semaphore_signal(barrier, inc=1, device_id=x_peer, device_id_type=MESH)

    local = []

    def bring(src, dst):
        copy = pltpu.make_async_copy(src, dst, local_sem.at[len(local)])
        copy.start()
        local.append(copy)

    bring(rows_ref, br)
    bring(stream_ref.at[pl.ds(pl.multiple_of(me * cap, cap), cap)], arr.at[pl.ds(pl.multiple_of(me * cap, cap), cap)])
    bring(w_query_ref, wq.at[t])
    bring(w_out_ref, wo)
    bring(w_in_ref, win.at[pl.ds(pl.multiple_of(me * depth, depth), depth)])
    bring(w_kv_ref, wkv.at[me])
    pl.semaphore_wait(barrier, n + 1)

    def remote(src, dst, send, arrive, where):
        return pltpu.make_async_remote_copy(
            src_ref=src, dst_ref=dst, send_sem=send, recv_sem=arrive, device_id=where, device_id_type=MESH
        )

    def held(kind, slot, h):
        if kind == 0:
            return win.at[pl.ds(pl.multiple_of(slot * depth + h * hd, hd), hd)]
        return wkv.at[slot, h, pl.ds((kind - 1) * hw, hw)]

    def own(kind, h):
        if kind == 0:
            return w_in_ref.at[pl.ds(pl.multiple_of(h * hd, hd), hd)]
        return w_kv_ref.at[h, pl.ds((kind - 1) * hw, hw)]

    def piece(kind, z, h, send, where, mine=False, core=None):
        slot = z * 2 + (d if core is None else core)
        dst = held(kind, slot, h)
        return remote(own(kind, h) if mine else dst, dst, send, recv.at[kind, slot, h], where)

    def right(kind, z, mine=False):
        return piece(kind, z, g, send_r.at[kind, z], {"seq": jnp.minimum(s + 1, n_seq - 1)}, mine)

    def left(kind, z, mine=False):
        return piece(kind, z, g, send_l.at[kind, z], {"seq": jnp.maximum(s - 1, 0)}, mine)

    def across(kind, z):
        return piece(kind, z, g, send_y.at[kind, z], y_peer)

    def core(kind, z, h, mine=False):
        return piece(kind, z, h, send_c.at[kind, z, h], c_peer, mine)

    def ends_of_line(kind):
        pl.when(s + 1 < n_seq)(lambda: right(kind, s, True).start())
        pl.when(s > 0)(lambda: left(kind, s, True).start())

    def each(k, fn):
        pl.when(s - k >= 0)(lambda: fn(s - k, True))
        pl.when(s + k < n_seq)(lambda: fn(s + k, False))

    def arrive(kind, k):
        def one(z, from_left):
            piece(kind, z, g, send_y.at[kind, z], y_peer).wait_recv()
            if from_left:
                pl.when(s + 1 < n_seq)(lambda: right(kind, z).start())
            else:
                pl.when(s > 0)(lambda: left(kind, z).start())
            across(kind, z).start()
            core(kind, z, g).start()
        each(k, one)

    def arrive_y(kind, k):
        def one(z, _):
            piece(kind, z, 1 - g, send_y.at[kind, z], y_peer).wait_recv()
            core(kind, z, 1 - g).start()
        each(k, one)

    def arrive_c(kind, k):
        def one(z, _=None):
            for h in range(2):
                piece(kind, z, h, send_c.at[kind, z, h], c_peer, core=1 - d).wait_recv()
        one(s) if k == 0 else each(k, one)

    ends_of_line(0)

    def stream_copy(i):
        b, where = other(i)
        src = stream_ref.at[pl.ds(pl.multiple_of(b * cap, cap), cap)]
        dst = arr.at[pl.ds(pl.multiple_of(me * cap, cap), cap)]
        return remote(src, dst, st_send.at[i], st_recv.at[i], where)

    for i in range(1, n):
        stream_copy(i).start()
    dh = dl // 2
    mine_rows = pl.ds(pl.multiple_of(d * dh, dh), dh)

    def x_copy(i):
        return remote(w_query_ref.at[mine_rows], wq.at[t, mine_rows], x_send.at[i], x_recv.at[i], x_peer)

    def xc_copy(i):
        dst = wq.at[1 - t, mine_rows]
        return remote(dst, dst, xc_send.at[i], xc_recv.at[i], c_peer)

    x_copy(0).start()
    for kind in range(3):
        for h in range(2):
            core(kind, s, h, True).start()
    ends_of_line(1)
    ends_of_line(2)

    local[0].wait()
    lens_row = lens_ref[...]
    tri = iota((count, count), 1) <= iota((count, count), 0)
    ends_col = jnp.sum(jnp.where(tri, lens_row, 0).astype(f32), axis=1, keepdims=True)
    lens_col = jnp.sum(
        jnp.where(iota((count, count), 0) == iota((count, count), 1), lens_row, 0).astype(f32), axis=1, keepdims=True
    )
    places = iota((count, byte_count), 1).astype(f32)
    members = jnp.where((places >= ends_col - lens_col) & (places < ends_col), 1.0, 0.0).astype(bf16)
    sums = jnp.dot(members, br[...], preferred_element_type=f32)
    pooled[pl.ds(0, count)] = (sums / lens_col).astype(bf16)
    _, following = other(1)
    halo_pooled = remote(
        pooled.at[pl.ds(count - HALO, HALO)], pooled.at[pl.ds(count, HALO)], h_send.at[0], h_recv.at[0], following
    )
    halo_pooled.start()

    arrive(0, 1)
    arrive(1, 1)
    x_copy(0).wait_recv()
    xc_copy(0).start()
    arrive(2, 1)
    arrive_y(0, 1)
    arrive(0, 2)
    local[2].wait()
    xc_copy(0).wait_recv()
    for part_t in range(2):
        query[:, part_t * cols:(part_t + 1) * cols] = jnp.dot(
            br[...], wq[part_t], preferred_element_type=f32
        ).astype(bf16) * (1.0 / math.sqrt(HEAD_DIM))
    arrive_y(1, 1)
    arrive(1, 2)
    arrive_y(2, 1)
    arrive(2, 2)
    arrive_y(0, 2)
    arrive(0, 3)

    for i in range(1, n):
        stream_copy(i).wait_recv()
    local[1].wait()
    owner = own_col_ref[...]
    same = (owner == own_row_ref[...]) & (iota((count, count), 1) < iota((count, count), 0))
    ranking = jnp.sum(jnp.where(same, 1.0, 0.0), axis=1, keepdims=True)
    target = owner.astype(f32) * cap + ranking
    pick = jnp.where(iota((count, n * cap), 1).astype(f32) == target, 1.0, 0.0).astype(bf16)
    mixed[pl.ds(0, count)] = jnp.dot(pick, arr[...], preferred_element_type=f32)
    hs_out[...] = mixed[pl.ds(count - HALO, HALO)].astype(bf16)
    halo_stream = remote(hs_out, hs_in, h_send.at[1], h_recv.at[1], following)
    halo_stream.start()
    arrive_y(1, 2)
    arrive_y(0, 3)
    for k in range(n_seq):
        arrive_c(0, k)
    local[4].wait()
    halo_pooled.wait_recv()
    halo_stream.wait_recv()
    mixed[pl.ds(count, HALO)] = hs_in[...].astype(f32)
    step = 512
    total = jnp.zeros((count + HALO, 128), f32)
    for c in range(width // step):
        at = pl.ds(c * step, step)
        now = mixed[:, at] + jnp.dot(pooled[...], win[:, at], preferred_element_type=f32)
        nrm[:, at] = (now * gain_ref[:, at]).astype(bf16)
        for j in range(step // 128):
            lane = now[:, j * 128:(j + 1) * 128]
            total = total + lane * lane
    sq[...] = total
    sq_copy = remote(sq, sq_in, p_send.at[n], p_recv.at[n], x_peer)
    sq_copy.start()

    def part_copy(slot):
        return remote(part_out.at[slot], part_in.at[slot], p_send.at[slot], p_recv.at[slot], x_peer)

    def project(z, _=None):
        for c in range(2):
            slot = z * 2 + c
            for h in range(2):
                val = jnp.dot(nrm[...], wkv[slot, h], preferred_element_type=f32)
                part[slot, :, pl.ds(h * 128, 128)] = val
                part_out[slot, :, pl.ds(h * 128, 128)] = val.astype(bf16)
            part_copy(slot).start()

    ends_row = jnp.dot(
        jnp.broadcast_to(lens_row.astype(f32), (8, count)).astype(bf16),
        jnp.where(iota((count, count), 0) <= iota((count, count), 1), 1.0, 0.0).astype(bf16),
        preferred_element_type=f32,
    )[0:1]
    keys_n = count + HALO
    key = iota((1, keys_n), 1)
    key = jnp.where(key < count, key, key - keys_n).astype(f32)
    for r in range(byte_count // ROWS):
        place = (iota((ROWS, 1), 0) + r * ROWS).astype(f32)
        patch = jnp.sum(jnp.where(ends_row <= place, 1.0, 0.0), axis=1, keepdims=True)
        floor = jnp.where(me == 0, jnp.maximum(patch - WIN, -1.0), patch - WIN)
        bias[pl.ds(r * ROWS, ROWS)] = jnp.where((key <= patch) & (key > floor), 0.0, -1e30)

    def attend(z, _=None):
        square = jnp.sum(sq[...] + sq_in[...], axis=1, keepdims=True)
        scale = lax.rsqrt(square / D + 1e-06)
        low_half = iota((keys_n, 128), 1) < HEAD_DIM
        for c in range(2):
            slot = z * 2 + c
            part_copy(slot).wait_recv()
            kv[slot] = ((part[slot] + part_in[slot].astype(f32)) * scale).astype(bf16)
            at = pl.ds(pl.multiple_of(slot * 128, 128), 128)
            keys, values = kv[slot, :, pl.ds(0, 128)], kv[slot, :, pl.ds(128, 128)]

            def chunk(r, carry):
                rows = pl.ds(pl.multiple_of(r * ROWS, ROWS), ROWS)
                q, shut = query[rows, at], bias[rows, :]
                result = jnp.zeros((ROWS, 128), f32)
                for low in (True, False):
                    pick_head = low_half if low else jnp.logical_not(low_half)
                    kh = jnp.where(pick_head, keys, jnp.zeros_like(keys))
                    vh = jnp.where(pick_head, values, jnp.zeros_like(values))
                    scores = lax.dot_general(q, kh, (((1,), (1,)), ((), ())), preferred_element_type=f32)
                    scores = scores + shut
                    expo = jnp.exp(scores - jnp.max(scores, axis=1, keepdims=True))
                    weights = (expo * (1.0 / jnp.sum(expo, axis=1, keepdims=True))).astype(bf16)
                    result = result + jnp.dot(weights, vh, preferred_element_type=f32)
                att[rows, at] = result.astype(bf16)
                return carry

            lax.fori_loop(0, byte_count // ROWS, chunk, 0)

    arrive(1, 3)
    arrive_y(2, 2)
    local[5].wait()
    arrive_c(1, 0)
    arrive_c(2, 0)
    project(s)
    arrive(2, 3)
    arrive_y(1, 3)
    arrive_c(1, 1)
    arrive_c(2, 1)
    each(1, project)
    sq_copy.wait_recv()
    arrive_c(1, 2)
    arrive_c(2, 2)
    arrive_y(2, 3)
    each(2, project)
    attend(s)
    each(1, attend)
    arrive_c(1, 3)
    arrive_c(2, 3)
    each(3, project)
    each(2, attend)
    each(3, attend)
    local[3].wait()
    my_cols = pl.ds(pl.multiple_of(t * cols, cols), cols)
    for r in range(byte_count // ROWS):
        rows = pl.ds(r * ROWS, ROWS)
        value = br[rows, my_cols].astype(f32) + jnp.dot(att[rows, :], wo[...], preferred_element_type=f32)
        out_ref[rows, :] = value.astype(bf16)

    for kind in range(3):
        pl.when(s + 1 < n_seq)(lambda: right(kind, s, True).wait_send())
        pl.when(s > 0)(lambda: left(kind, s, True).wait_send())
        for h in range(2):
            core(kind, s, h, True).wait_send()
        for k in range(1, n_seq):
            def sent(z, from_left):
                if from_left:
                    pl.when(s + 1 < n_seq)(lambda: right(kind, z).wait_send())
                else:
                    pl.when(s > 0)(lambda: left(kind, z).wait_send())
                across(kind, z).wait_send()
                core(kind, z, 0).wait_send()
                core(kind, z, 1).wait_send()
            each(k, sent)
    for i in range(1, n):
        stream_copy(i).wait_send()
    x_copy(0).wait_send()
    xc_copy(0).wait_send()
    halo_pooled.wait_send()
    halo_stream.wait_send()
    sq_copy.wait_send()
    lax.fori_loop(0, n, lambda slot, carry: (part_copy(slot).wait_send(), carry)[1], 0)


def fused(
    byte_rows, patch_lengths, patch_owner, patch_stream, w_in, norm_gain, w_kv, w_query, w_out
):
    n_seq = lax.axis_size("seq")
    n = n_seq * 2
    byte_count, dl = byte_rows.shape
    count = patch_owner.shape[0]
    depth, width = w_in.shape
    cols = w_query.shape[1]
    tall = count + HALO
    any_spec, vmem = pl.BlockSpec(memory_space=pl.ANY), pl.BlockSpec(memory_space=pltpu.VMEM)
    dma = pltpu.SemaphoreType.DMA
    return pl.pallas_call(
        functools.partial(fused_kernel, n_seq),
        out_shape=jax.ShapeDtypeStruct((byte_count, cols), bf16),
        in_specs=[any_spec, vmem, vmem, vmem, any_spec, any_spec, vmem, any_spec, any_spec, any_spec],
        out_specs=vmem,
        scratch_shapes=[
            pltpu.VMEM((n * depth, width), bf16),
            pltpu.VMEM((n, 2, width, 128), bf16),
            pltpu.VMEM(patch_stream.shape, bf16),
            pltpu.VMEM((byte_count, dl), bf16),
            pltpu.VMEM((2, dl, cols), bf16),
            pltpu.VMEM((dl, cols), bf16),
            pltpu.VMEM((tall, dl), bf16),
            pltpu.VMEM((tall, width), f32),
            pltpu.VMEM((tall, width), bf16),
            pltpu.VMEM((HALO, width), bf16),
            pltpu.VMEM((HALO, width), bf16),
            pltpu.VMEM((n, tall, 256), f32),
            pltpu.VMEM((n, tall, 256), bf16),
            pltpu.VMEM((n, tall, 256), bf16),
            pltpu.VMEM((n, tall, 256), bf16),
            pltpu.VMEM((tall, 128), f32),
            pltpu.VMEM((tall, 128), f32),
            pltpu.VMEM((byte_count, dl), bf16),
            pltpu.VMEM((byte_count, dl), bf16),
            pltpu.VMEM((byte_count, tall), f32),
            dma((3, n, 2)),
            dma((3, n_seq)),
            dma((3, n_seq)),
            dma((3, n_seq)),
            dma((3, n_seq, 2)),
            dma((6,)),
            dma((n,)),
            dma((n,)),
            dma((2,)),
            dma((2,)),
            dma((2,)),
            dma((2,)),
            dma((2,)),
            dma((2,)),
            dma((n + 1,)),
            dma((n + 1,)),
        ],
        compiler_params=pltpu.CompilerParams(
            collective_id=0, has_side_effects=True, vmem_limit_bytes=56 * 1024 * 1024
        ),
        cost_estimate=pl.CostEstimate(flops=9 * 10**9, bytes_accessed=8 * 10**6, transcendentals=2 * 10**6),
    )(
        byte_rows, patch_lengths, patch_owner, patch_owner.reshape(1, count), patch_stream, w_in,
        norm_gain.reshape(1, width), w_kv, w_query, w_out,
    )


def solution(mesh):
    sizes = mesh.shape
    fits = sizes["groups"] == 2 and sizes["tp"] == 2 and sizes["dp"] == 2 and sizes["seq"] == 4
    return jax.shard_map(
        fused if fits else local,
        mesh=mesh,
        in_specs=(
            P(("groups", "seq", "dp"), None),
            P(("groups", "seq", "dp"), None),
            P(("groups", "seq", "dp"), None),
            P(("groups", "seq", "dp"), "tp"),
            P(("seq", "dp"), "tp"),
            P("tp"),
            P(None, "tp", ("seq", "dp")),
            P(None, "tp"),
            P(None, "tp"),
        ),
        out_specs=P(("groups", "seq", "dp"), "tp"),
        check_vma=False,
    )
```
